32 devices in a mesh: wide: 16 (over z, y, core), narrow: 2 (over x).
Axes of the slice: x: 2, y: 2, z: 4, core: 2. Of those that a mesh axis runs over, the one named last changes fastest.
Arguments:
- hidden_in: bfloat16 [16384, 768], P('wide'), may hold values from -6 to 6
- image_tokens: bfloat16 [128, 256, 768], P('wide', 'narrow'), may hold values from -6 to 6
- image_group: int32 [256], P('wide'), may hold values from 0 to 127, as said below
- caption_len: int32 [256], P('wide'), may hold values from 16 to 64, as said below
- norm_gain: bfloat16 [3, 768], replicated, may hold values from 0.25 to 1.75
- norm_bias: bfloat16 [3, 768], replicated, may hold values from -1 to 1
- self_qkv: bfloat16 [768, 2304], replicated, may hold values from -0.3125 to 0.3125
- self_out: bfloat16 [768, 768], replicated, may hold values from -0.4375 to 0.4375
- cross_query: bfloat16 [768, 768], replicated, may hold values from -0.3125 to 0.3125
- cross_kv: bfloat16 [768, 1536], replicated, may hold values from -0.3125 to 0.3125
- cross_out: bfloat16 [768, 768], replicated, may hold values from -0.875 to 0.875
- mlp_in: bfloat16 [768, 3072], replicated, may hold values from -0.21875 to 0.21875
- mlp_bias_in: bfloat16 [3072], replicated, may hold values from -3 to 3
- mlp_out: bfloat16 [3072, 768], replicated, may hold values from -0.109375 to 0.109375
- mlp_bias_out: bfloat16 [768], replicated, may hold values from -2 to 2
- out_grad: bfloat16 [16384, 768], P('wide'), may hold values from -6 to 6
Outputs:
- hidden_out: bfloat16 [16384, 768], P(('wide', 'narrow'))
- grad_hidden: float32 [16384, 768], P(('wide', 'narrow'))
- grad_image: float32 [128, 256, 768], P('wide', 'narrow')
- grad_norm_gain: float32 [3, 768], P(None, 'narrow')
- grad_norm_bias: float32 [3, 768], P(None, 'narrow')
- grad_self_qkv: float32 [768, 2304], P('narrow')
- grad_self_out: float32 [768, 768], P('narrow')
- grad_cross_query: float32 [768, 768], P('narrow')
- grad_cross_kv: float32 [768, 1536], P('narrow')
- grad_cross_out: float32 [768, 768], P('narrow')
- grad_mlp_in: float32 [768, 3072], P('narrow')
- grad_mlp_bias_in: float32 [3072], P('narrow')
- grad_mlp_out: float32 [3072, 768], P('narrow')
- grad_mlp_bias_out: float32 [768], P('narrow')
The draws below stay inside these ranges and needn't reach their ends.
Inputs may be any that keep to these rules, and one draw needn't show every extreme that they name: `image_group`: each image is named by exactly two captions. The captions of one index of wide, an aligned block of 16, name only the 8 images of that index. `caption_len`: in every aligned block of 16 captions one caption has 64 valid tokens and one has 16.
All inputs are finite; a program needn't handle non-finite values.
Results may differ from the reference program's by a relative error of at most 0.033.
Values may be sent and summed in bfloat16 or wider, within the bound.
No kernel may reach another device: no remote copies, remote signals or barrier semaphores. Data moves between devices by JAX's collectives and lax.ppermute only.
A program may use at most 256 MiB of HBM per device.

```python
import math
import jax
import jax.numpy as jnp
from jax import lax

D = 768
HEADS = 12
HEAD_DIM = 64
FF = 3072
IMG_TOK = 256
SEQ = 64
PAIRS_DEV = 8
CAPTIONS = 256
IMAGES = 128
TOKENS = 16384


def block_permute(sub_key):
    return jax.random.permutation(sub_key, 2 * PAIRS_DEV)


def block_orders(key):
    block_count = CAPTIONS // (2 * PAIRS_DEV)
    return jax.vmap(block_permute)(jax.random.split(key, block_count))


def draw_image_group(key, part):
    key = jax.random.fold_in(key, 11)
    ordering = block_orders(key)
    block_count = CAPTIONS // (2 * PAIRS_DEV)
    offsets = jnp.arange(block_count, dtype=jnp.int32)[:, None] * PAIRS_DEV
    return (ordering // 2 + offsets).reshape(-1).astype(jnp.int32)


def draw_caption_len(key, part):
    key = jax.random.fold_in(key, 23)
    ordering = block_orders(jax.random.fold_in(key, 1))
    block_count = CAPTIONS // (2 * PAIRS_DEV)
    spread = jax.random.randint(jax.random.fold_in(key, 2), (block_count, 2 * PAIRS_DEV), SEQ // 4, SEQ + 1)
    lengths = jnp.where(ordering == 0, SEQ, jnp.where(ordering == 1, SEQ // 4, spread))
    return lengths.reshape(-1).astype(jnp.int32)


def block_scale(stream_key, extent, cuts, low, high):
    factor_of = 1.0
    for position, blocks in cuts:
        steps = jax.random.uniform(jax.random.fold_in(jax.random.fold_in(stream_key, 6), position), (blocks,), jnp.float32, low / len(cuts), high / len(cuts))
        factor_of = factor_of * jnp.repeat(jnp.exp(steps), extent[position] // blocks).reshape((-1,) + (1,) * (len(extent) - 1 - position))
    return factor_of


def gaussian(key, dims, scale, most, pieces=(), kind=jnp.bfloat16):
    gain = block_scale(key, dims, pieces, -0.22, 0.18) if pieces else 1.0
    entries = jax.random.normal(key, dims, jnp.float32) * scale * gain
    return jnp.minimum(jnp.maximum(entries, -most), most).astype(kind)


def setup_inputs(seed: int = 0) -> dict:
    seeds = jax.random.split(jax.random.key(seed), 17)
    return {
        "hidden_in": gaussian(seeds[0], (TOKENS, D), 1.0, 6.0, ((0, 16),)),
        "image_tokens": gaussian(seeds[1], (IMAGES, IMG_TOK, D), 1.0, 6.0, ((0, 16), (1, 2))),
        "image_group": draw_image_group(jax.random.fold_in(seeds[16], 71), 0),
        "caption_len": draw_caption_len(jax.random.fold_in(seeds[16], 71), 0),
        "norm_gain": jnp.clip(1.0 + 0.15 * jax.random.normal(seeds[4], (3, D), jnp.float32), 0.25, 1.75).astype(jnp.bfloat16),
        "norm_bias": gaussian(seeds[5], (3, D), 0.2, 1.0),
        "self_qkv": gaussian(seeds[6], (D, 3 * D), (D // 2) ** -0.5, 0.3125),
        "self_out": gaussian(seeds[7], (D, D), (D // 4) ** -0.5, 0.4375),
        "cross_query": gaussian(seeds[8], (D, D), (D // 2) ** -0.5, 0.3125),
        "cross_kv": gaussian(seeds[9], (D, 2 * D), (D // 2) ** -0.5, 0.3125),
        "cross_out": gaussian(seeds[10], (D, D), (D // 16) ** -0.5, 0.875),
        "mlp_in": gaussian(seeds[11], (D, FF), D ** -0.5, 0.21875),
        "mlp_bias_in": gaussian(seeds[12], (FF,), 0.5, 3.0),
        "mlp_out": gaussian(seeds[13], (FF, D), FF ** -0.5, 0.109375),
        "mlp_bias_out": gaussian(seeds[14], (D,), 0.3, 2.0),
        "out_grad": gaussian(seeds[15], (TOKENS, D), 1.0, 6.0, ((0, 16),)),
    }


@jax.custom_vjp
def low(v):
    return lax.optimization_barrier(v.astype(jnp.bfloat16)).astype(jnp.float32)

@jax.custom_vjp
def low_back(v):
    return v

def low_keep(v):
    return (low(v), None)

def low_pass(kept, grad):
    return (grad,)

def back_keep(v):
    return (v, None)

def back_low(kept, grad):
    return (low(grad),)
low.defvjp(low_keep, low_pass)
low_back.defvjp(back_keep, back_low)

def apply_layer_norm(values, gain_row, shift_row):
    center = values - lax.optimization_barrier(jnp.mean(values, axis=-1, keepdims=True))
    return center * lax.rsqrt(lax.optimization_barrier(jnp.mean(center * center, axis=-1, keepdims=True)) + 1e-05) * gain_row + shift_row

def mat_mul(left, right):
    return jnp.dot(left, right, precision=lax.Precision.HIGHEST)

def caption_block(block_in, block_group, block_len, params, image_kv):
    layer_norm_gains, layer_norm_shifts, w_qkv, w_self_out, w_query, w_cross_out, w_in, bias_in, w_out, bias_out = params
    block_rows = block_in.shape[0]
    block_caps = block_rows // SEQ
    score_scale = HEAD_DIM ** (-0.5)
    positions = jnp.arange(SEQ)
    allowed = (positions[:, None] >= positions[None, :])[None] & (positions[None, None, :] < block_len[:, None, None])
    attn_input = low(apply_layer_norm(block_in, layer_norm_gains[0], layer_norm_shifts[0]))
    qkv_all = low(low_back(mat_mul(attn_input, w_qkv))).reshape(block_caps, SEQ, 3, HEADS, HEAD_DIM)
    self_logits = low_back(jnp.einsum('cqhd,ckhd->chqk', qkv_all[:, :, 0], qkv_all[:, :, 1], precision=lax.Precision.HIGHEST) * score_scale)
    self_probs = low(jax.nn.softmax(jnp.where(allowed[:, None], self_logits, -1e+30), axis=-1))
    self_mix = low(low_back(jnp.einsum('chqk,ckhd->cqhd', self_probs, qkv_all[:, :, 2], precision=lax.Precision.HIGHEST))).reshape(block_rows, D)
    first_residual_stream = block_in + low_back(mat_mul(self_mix, w_self_out))
    cross_input = low(apply_layer_norm(first_residual_stream, layer_norm_gains[1], layer_norm_shifts[1]))
    cross_q = low(low_back(mat_mul(cross_input, w_query))).reshape(block_caps, SEQ, HEADS, HEAD_DIM)
    caption_kv = image_kv[block_group]
    cross_logits = low_back(jnp.einsum('cqhd,ckhd->chqk', cross_q, caption_kv[:, :, 0], precision=lax.Precision.HIGHEST) * score_scale)
    cross_probs = low(jax.nn.softmax(cross_logits, axis=-1))
    cross_mix = low(low_back(jnp.einsum('chqk,ckhd->cqhd', cross_probs, caption_kv[:, :, 1], precision=lax.Precision.HIGHEST))).reshape(block_rows, D)
    second_residual_stream = first_residual_stream + low_back(mat_mul(cross_mix, w_cross_out))
    mlp_input = low(apply_layer_norm(second_residual_stream, layer_norm_gains[2], layer_norm_shifts[2]))
    pre_act = low_back(mat_mul(mlp_input, w_in) + bias_in)
    activated = low(jax.nn.gelu(pre_act, approximate=False))
    return second_residual_stream + low_back(mat_mul(activated, w_out) + bias_out)

def reference(hidden_in, image_tokens, image_group, caption_len, norm_gain, norm_bias, self_qkv, self_out, cross_query, cross_kv, cross_out, mlp_in, mlp_bias_in, mlp_out, mlp_bias_out, out_grad):
    block_caps = math.gcd(CAPTIONS, 32)
    block_count = CAPTIONS // block_caps
    group_blocks = image_group.reshape(block_count, block_caps).astype(jnp.int32)
    length_blocks = caption_len.reshape(block_count, block_caps).astype(jnp.int32)

    def forward(hidden, images, layer_norm_gains, layer_norm_shifts, w_qkv, w_self_out, w_query, w_kv, w_cross_out, w_in, bias_in, w_out, bias_out):
        image_kv = low(low_back(jnp.einsum('itd,de->ite', images, w_kv, precision=lax.Precision.HIGHEST)))
        image_kv = image_kv.reshape(IMAGES, IMG_TOK, 2, HEADS, HEAD_DIM)
        params = (layer_norm_gains, layer_norm_shifts, w_qkv, w_self_out, w_query, w_cross_out, w_in, bias_in, w_out, bias_out)

        def one_block(operands):
            return caption_block(operands[0], operands[1], operands[2], params, image_kv)
        blocks_out = lax.map(jax.checkpoint(one_block), (hidden.reshape(block_count, block_caps * SEQ, D), group_blocks, length_blocks))
        return blocks_out.reshape(TOKENS, D)
    primals = tuple((operand.astype(jnp.float32) for operand in (hidden_in, image_tokens, norm_gain, norm_bias, self_qkv, self_out, cross_query, cross_kv, cross_out, mlp_in, mlp_bias_in, mlp_out, mlp_bias_out)))
    result, pull_back = jax.vjp(forward, *primals)
    grads = pull_back(out_grad.astype(jnp.float32))
    return (result.astype(jnp.bfloat16), grads[0], grads[1], grads[2], grads[3], grads[4], grads[5], grads[6], grads[7], grads[8], grads[9], grads[10], grads[11], grads[12])
```

```python
import functools

import jax
import jax.numpy as jnp
from jax import lax
from jax.experimental import pallas as pl
from jax.experimental.pallas import tpu as pltpu
from jax.sharding import PartitionSpec as P

D = 768
HEADS = 12
HEAD_DIM = 64
FF = 3072
SEQ = 64
IMG_TOK = 256
PAIRS = HEADS // 2
SCALE = HEAD_DIM**-0.5
BLOCK = 48
BLOCKS = D // BLOCK
WIDE_COLS = 2 * D
TILE = 256
f32 = jnp.float32
bf16 = jnp.bfloat16
VM = pl.BlockSpec(memory_space=pltpu.VMEM)
SM = pl.BlockSpec(memory_space=pltpu.SMEM)
CAPS, LENS, MINE, PEER, IMG_SRC, OUT_SRC, FLIP, CORE, PLAN = 0, 8, 16, 20, 24, 32, 40, 41, 48


def mm(left, right):
    return lax.dot_general(left, right, (((1,), (0,)), ((), ())), preferred_element_type=f32)


def mm_nt(left, right):
    return lax.dot_general(left, right, (((1,), (1,)), ((), ())), preferred_element_type=f32)


def mm_tn(left, right):
    return lax.dot_general(left, right, (((0,), (0,)), ((), ())), preferred_element_type=f32)


def params(vmem=56, grid=None):
    return pltpu.CompilerParams(
        vmem_limit_bytes=vmem * 1024 * 1024,
        dimension_semantics=None if grid is None else ("arbitrary",) * grid,
    )


def cost(flops, nbytes, trans=0):
    return pl.CostEstimate(flops=int(flops), bytes_accessed=int(nbytes), transcendentals=int(trans))


def sds(shape, dtype):
    return jax.ShapeDtypeStruct(shape, dtype)


def normed(x):
    center = x - jnp.mean(x, axis=-1, keepdims=True)
    inv = lax.rsqrt(jnp.mean(center * center, axis=-1, keepdims=True) + 1e-05)
    return center * inv, inv


def norm_back(grad, xhat, inv, gain):
    u = grad * gain
    return inv * (
        u - jnp.mean(u, axis=-1, keepdims=True) - xhat * jnp.mean(u * xhat, axis=-1, keepdims=True)
    )


def lane_masks(scale):
    lane = lax.broadcasted_iota(jnp.int32, (1, 2 * HEAD_DIM), 1)
    low = jnp.where(lane < HEAD_DIM, scale, 0.0).astype(bf16)
    high = jnp.where(lane < HEAD_DIM, 0.0, scale).astype(bf16)
    return low, high


def two_heads(x, masks):
    return jnp.concatenate([x * masks[0], x * masks[1]], axis=0)


def join_heads(x, rows):
    lane = lax.broadcasted_iota(jnp.int32, (rows, 2 * HEAD_DIM), 1)
    return jnp.where(lane < HEAD_DIM, x[:rows], x[rows:])


def plan_kernel(narrow, images, group, lens, pos, out, place, count):
    me = pos[0]
    base = pos[1]
    half = images // narrow
    caps = 2 * images
    for p in range(images):
        count[p] = 0
    for c in range(caps):
        g = group[c] - base
        n = count[g]
        place[2 * g + n] = c
        count[g] = n + 1
    for i in range(PLAN):
        out[i] = 0
    out[FLIP] = pos[2]
    out[CORE] = pos[3]
    slots = [jnp.int32(0) for _ in range(2)]
    turn = jnp.int32(0)
    for p in range(images):
        a = place[2 * p]
        b = place[2 * p + 1]
        if narrow == 2:
            both_low = b < images
            both_high = a >= images
            mixed = jnp.logical_not(jnp.logical_or(both_low, both_high))
            owner = jnp.where(both_low, 0, jnp.where(both_high, 1, turn))
            turn = jnp.where(mixed, 1 - turn, turn)
            slot = jnp.where(owner == 0, slots[0], slots[1])
            slots[0] = jnp.where(owner == 0, slots[0] + 1, slots[0])
            slots[1] = jnp.where(owner == 1, slots[1] + 1, slots[1])
            swap = jnp.logical_and(mixed, owner == 1)
            first = jnp.where(swap, b, a)
            second = jnp.where(swap, a, b)
            mine = owner == me

            @pl.when(mine)
            def _():
                out[MINE + slot] = p
                out[CAPS + 2 * slot] = first
                out[CAPS + 2 * slot + 1] = second
                out[LENS + 2 * slot] = lens[first]
                out[LENS + 2 * slot + 1] = lens[second]

            @pl.when(jnp.logical_not(mine))
            def _():
                out[PEER + slot] = p

            out[IMG_SRC + p] = jnp.where(mine, slot, half + slot)
            for k, c in ((0, first), (1, second)):

                @pl.when(c // images == me)
                def _():
                    out[OUT_SRC + c - me * images] = jnp.where(mine, 2 * slot + k, caps // 2 + slot)

        else:
            owner = p // half
            slot = p % half
            mine = owner == me
            per = caps // narrow

            @pl.when(mine)
            def _():
                out[MINE + slot] = p
                for k, c in ((0, a), (1, b)):
                    out[CAPS + 2 * slot + k] = c
                    out[LENS + 2 * slot + k] = lens[c]

            for k, c in ((0, a), (1, b)):

                @pl.when(c // per == me)
                def _():
                    out[OUT_SRC + c - me * per] = 2 * p + k


def make_plan(narrow, images, group, lens, pos):
    return pl.pallas_call(
        functools.partial(plan_kernel, narrow, images),
        out_shape=sds((PLAN,), jnp.int32),
        in_specs=[SM, SM, SM],
        out_specs=SM,
        scratch_shapes=[
            pltpu.SMEM((2 * images,), jnp.int32),
            pltpu.SMEM((images,), jnp.int32),
        ],
        compiler_params=params(4),
        name="plan",
    )(group, lens, pos)


def pick_kernel(plan, tokens_a, tokens_b, mine, peer):
    mine[...] = tokens_a[...]
    peer[...] = tokens_b[...]


def pick_tokens(plan, tokens, count):
    block = (1,) + tokens.shape[1:]
    return pl.pallas_call(
        pick_kernel,
        grid_spec=pltpu.PrefetchScalarGridSpec(
            num_scalar_prefetch=1,
            grid=(count,),
            in_specs=[
                pl.BlockSpec(block, lambda i, plan: (plan[MINE + i], 0, 0)),
                pl.BlockSpec(block, lambda i, plan: (plan[PEER + i], 0, 0)),
            ],
            out_specs=[pl.BlockSpec(block, lambda i, plan: (i, 0, 0))] * 2,
        ),
        out_shape=[sds((count,) + tokens.shape[1:], bf16)] * 2,
        compiler_params=params(8),
        name="pick",
    )(plan, tokens, tokens)


def place_kernel(offset, count, plan, own, got, out):
    have = own.shape[0]
    for i in range(count):
        src = plan[offset + i]

        @pl.when(src < have)
        def _():
            out[i] = own[jnp.minimum(src, have - 1)].astype(out.dtype)

        @pl.when(src >= have)
        def _():
            out[i] = got[jnp.maximum(src - have, 0)].astype(out.dtype)


def place(offset, count, plan, own, got, dtype, name):
    return pl.pallas_call(
        functools.partial(place_kernel, offset, count),
        out_shape=sds((count,) + own.shape[1:], dtype),
        in_specs=[SM, VM, VM],
        out_specs=VM,
        compiler_params=params(24),
        cost_estimate=cost(0, 4 * count * own.shape[1] * own.shape[2] * 2),
        name=name,
    )(plan, own, got)


def front_kernel(
    plan, hidden, out_grad, gain, bias, w_qkv, w_self, w_query,
    x_out, g_out, attn_out, qkv_out, probs_out, mix_out, one_out, cin_out, cq_out,
):
    rows = x_out.shape[0]
    gain0, bias0 = gain[0:1, :].astype(f32), bias[0:1, :].astype(f32)
    gain1, bias1 = gain[1:2, :].astype(f32), bias[1:2, :].astype(f32)

    def gather(i, _):
        src = pl.ds(pl.multiple_of(plan[CAPS + i] * SEQ, SEQ), SEQ)
        dst = pl.ds(pl.multiple_of(i * SEQ, SEQ), SEQ)
        x = hidden[src, :]
        x_out[dst, :] = x
        g_out[dst, :] = out_grad[src, :]
        attn_out[dst, :] = (normed(x.astype(f32))[0] * gain0 + bias0).astype(bf16)
        return 0

    lax.fori_loop(0, rows // SEQ, gather, 0)
    for j in range(3):
        cols = slice(j * D, (j + 1) * D)
        qkv_out[:, cols] = mm(attn_out[...], w_qkv[:, cols]).astype(bf16)
    masks = lane_masks(SCALE)
    row = lax.broadcasted_iota(jnp.int32, (2 * SEQ, 2 * SEQ), 0)
    col = lax.broadcasted_iota(jnp.int32, (2 * SEQ, 2 * SEQ), 1)
    causal = jnp.logical_and(col <= row, (col // SEQ) == (row // SEQ))

    def attend(p, _):
        span = pl.ds(pl.multiple_of(p * 2 * SEQ, 2 * SEQ), 2 * SEQ)
        length = jnp.where(col < SEQ, plan[LENS + 2 * p], plan[LENS + 2 * p + 1])
        allowed = jnp.logical_and(causal, (col % SEQ) < length)
        fill = jnp.where(allowed, 0.0, -1e30)
        fill = jnp.concatenate([fill, fill], axis=0)
        for h in range(PAIRS):
            at = 2 * HEAD_DIM * h
            q = two_heads(qkv_out[span, at : at + 128], masks)
            k = qkv_out[span, D + at : D + at + 128]
            v = qkv_out[span, 2 * D + at : 2 * D + at + 128]
            logits = jnp.where(fill < 0.0, fill, mm_nt(q, k))
            e = jnp.exp(logits - jnp.max(logits, axis=-1, keepdims=True))
            low = (e * (1.0 / jnp.sum(e, axis=-1, keepdims=True))).astype(bf16)
            probs_out[p, h] = low
            mix_out[span, at : at + 128] = join_heads(mm(low, v), 2 * SEQ).astype(bf16)
        return 0

    lax.fori_loop(0, rows // (2 * SEQ), attend, 0)
    one_out[...] = mm(mix_out[...], w_self[...])

    def second(i, _):
        span = pl.ds(pl.multiple_of(i * SEQ, SEQ), SEQ)
        one = one_out[span, :] + x_out[span, :].astype(f32)
        one_out[span, :] = one
        cin_out[span, :] = (normed(one)[0] * gain1 + bias1).astype(bf16)
        return 0

    lax.fori_loop(0, rows // SEQ, second, 0)
    cq_out[...] = mm(cin_out[...], w_query[...]).astype(bf16)


def front(rows, plan, hidden, out_grad, gain, bias, w_qkv, w_self, w_query):
    pairs = rows // (2 * SEQ)
    return pl.pallas_call(
        front_kernel,
        out_shape=[
            sds((rows, D), bf16),
            sds((rows, D), bf16),
            sds((rows, D), bf16),
            sds((rows, 3 * D), bf16),
            sds((pairs, PAIRS, 4 * SEQ, 2 * SEQ), bf16),
            sds((rows, D), bf16),
            sds((rows, D), f32),
            sds((rows, D), bf16),
            sds((rows, D), bf16),
        ],
        in_specs=[SM] + [VM] * 7,
        out_specs=[VM] * 9,
        compiler_params=params(),
        cost_estimate=cost(rows * D * D * 10 * 2, 24e6, rows * 2 * D),
        name="front",
    )(plan, hidden, out_grad, gain, bias, w_qkv, w_self, w_query)


def cross_kernel(tokens, cq, one, gain, bias, w_kv, w_cross, kv_out, probs_out, mix_out, two_out, min_out):
    rows = cq.shape[0]
    images = rows // (2 * SEQ)
    gain2, bias2 = gain[2:3, :].astype(f32), bias[2:3, :].astype(f32)
    for j in range(2):
        cols = slice(j * D, (j + 1) * D)
        kv_out[:, cols] = mm(tokens[...], w_kv[:, cols]).astype(bf16)
    masks = lane_masks(SCALE)

    def attend(p, _):
        span = pl.ds(pl.multiple_of(p * 2 * SEQ, 2 * SEQ), 2 * SEQ)
        toks = pl.ds(pl.multiple_of(p * IMG_TOK, IMG_TOK), IMG_TOK)
        for h in range(PAIRS):
            at = 2 * HEAD_DIM * h
            q = two_heads(cq[span, at : at + 128], masks)
            logits = mm_nt(q, kv_out[toks, at : at + 128])
            e = jnp.exp(logits - jnp.max(logits, axis=-1, keepdims=True))
            low = (e * (1.0 / jnp.sum(e, axis=-1, keepdims=True))).astype(bf16)
            probs_out[p, h] = low
            mix = mm(low, kv_out[toks, D + at : D + at + 128])
            mix_out[span, at : at + 128] = join_heads(mix, 2 * SEQ).astype(bf16)
        return 0

    lax.fori_loop(0, images, attend, 0)
    two_out[...] = mm(mix_out[...], w_cross[...])

    def second(i, _):
        span = pl.ds(pl.multiple_of(i * SEQ, SEQ), SEQ)
        two = two_out[span, :] + one[span, :]
        two_out[span, :] = two
        min_out[span, :] = (normed(two)[0] * gain2 + bias2).astype(bf16)
        return 0

    lax.fori_loop(0, rows // SEQ, second, 0)


def cross(tokens, cq, one, gain, bias, w_kv, w_cross):
    rows = cq.shape[0]
    images = rows // (2 * SEQ)
    return pl.pallas_call(
        cross_kernel,
        out_shape=[
            sds((tokens.shape[0], 2 * D), bf16),
            sds((images, PAIRS, 4 * SEQ, IMG_TOK), bf16),
            sds((rows, D), bf16),
            sds((rows, D), f32),
            sds((rows, D), bf16),
        ],
        in_specs=[VM] * 7,
        out_specs=[VM] * 5,
        compiler_params=params(),
        cost_estimate=cost(rows * D * D * 8 * 2, 20e6, rows * 4 * D),
        name="cross",
    )(tokens, cq, one, gain, bias, w_kv, w_cross)


def store_split(core, keep, send, first, second):
    @pl.when(core == 0)
    def _():
        first(keep)
        second(send)

    @pl.when(core == 1)
    def _():
        first(send)
        second(keep)


def mlp_kernel(
    plan, min_ref, g_ref, acc_in, gn_in, w_in, b_in, w_out,
    acc, gn, keep, send, gbias, min_t,
):
    step = pl.program_id(0)
    flip = plan[FLIP]

    @pl.when(step == 0)
    def _():
        acc[...] = acc_in[...]
        gn[...] = gn_in[...]
        min_t[...] = min_ref[...].T

    pre = mm(min_ref[...], w_in[...]) + b_in[...].astype(f32)
    phi = 0.5 + 0.5 * lax.erf(pre * (2.0**-0.5))
    act = (pre * phi).astype(bf16)
    slope = phi + pre * jnp.exp(-0.5 * pre * pre) * 0.3989422804014327
    acc[...] += mm(act, w_out[...])
    grad_pre = slope * mm_nt(g_ref[...], w_out[...])
    gbias[...] = jnp.sum(grad_pre, axis=0, keepdims=True)
    low = grad_pre.astype(bf16)
    gn[...] += mm_nt(low, w_in[...])
    grad_in = mm(min_t[...], low).astype(bf16)
    grad_out = mm_tn(act, g_ref[...]).astype(bf16)
    cols = pl.ds(pl.multiple_of(step * TILE, TILE), TILE)
    half = step // 3
    spot = pl.ds(pl.multiple_of((step % 3) * 16, 16), 16)

    def first(ref):
        for b in range(BLOCKS):
            ref[b ^ flip, :, cols] = grad_in[b * BLOCK : (b + 1) * BLOCK, :]

    def second(ref):
        for w in range(8):
            slot = (half * 8 + w) ^ flip
            ref[slot, spot, 0:D] = grad_out[w * 32 : w * 32 + 16, :]
            ref[slot, spot, D : 2 * D] = grad_out[w * 32 + 16 : w * 32 + 32, :]

    store_split(plan[CORE], keep, send, first, second)


def mlp(call, plan, min_, g, acc, gn, w_in, b_in, w_out):
    rows = g.shape[0]
    tile = lambda k: k + 3 * (k // 3) + 3 * call
    whole = lambda *shape: pl.BlockSpec(shape, lambda k: (0,) * len(shape))
    return pl.pallas_call(
        mlp_kernel,
        grid=(6,),
        out_shape=[
            sds((rows, D), f32),
            sds((rows, D), f32),
            sds((BLOCKS, BLOCK, WIDE_COLS), bf16),
            sds((BLOCKS, BLOCK, WIDE_COLS), bf16),
            sds((1, 6 * TILE), f32),
        ],
        in_specs=[
            SM,
            whole(rows, D),
            whole(rows, D),
            whole(rows, D),
            whole(rows, D),
            pl.BlockSpec((D, TILE), lambda k: (0, tile(k))),
            pl.BlockSpec((1, TILE), lambda k: (0, tile(k))),
            pl.BlockSpec((TILE, D), lambda k: (tile(k), 0)),
        ],
        out_specs=[
            whole(rows, D),
            whole(rows, D),
            whole(BLOCKS, BLOCK, WIDE_COLS),
            whole(BLOCKS, BLOCK, WIDE_COLS),
            pl.BlockSpec((1, TILE), lambda k: (0, k)),
        ],
        scratch_shapes=[pltpu.VMEM((D, rows), bf16)],
        compiler_params=params(56, 1),
        cost_estimate=cost(rows * D * 6 * TILE * 12, 20e6, rows * 6 * TILE * 2),
        name="mlp",
    )(plan, min_, g, acc, gn, w_in, b_in.reshape(1, FF), w_out)


def store_blocks(ref, flip, cols, value):
    for b in range(BLOCKS):
        ref[b ^ flip, :, cols] = value[b * BLOCK : (b + 1) * BLOCK, :]


def cross_back_kernel(
    plan, acc, gn, two, one, g, gain, b_out, w_cross, w_query, w_kv, mix, probs, kv, cq, cin, tokens,
    hid_out, keep, send, gone_out, gimg_out, small_out, gtwo, low, gmix, gcq, gkv,
):
    rows = cq.shape[0]
    images = rows // (2 * SEQ)
    flip = plan[FLIP]
    core = plan[CORE]
    gain1, gain2 = gain[1:2, :].astype(f32), gain[2:3, :].astype(f32)
    bias_out = b_out[...].astype(f32)
    small_out[...] = jnp.zeros_like(small_out)

    def top(i, _):
        span = pl.ds(pl.multiple_of(i * SEQ, SEQ), SEQ)
        x = two[span, :]
        hid_out[i] = (x + (acc[span, :] + bias_out)).astype(bf16)
        up = g[span, :].astype(f32)
        grad = gn[span, :]
        xhat, inv = normed(x)
        small_out[0:1, :] += jnp.sum(grad * xhat, axis=0, keepdims=True)
        small_out[1:2, :] += jnp.sum(grad, axis=0, keepdims=True)
        small_out[4:5, :] += jnp.sum(up, axis=0, keepdims=True)
        total = up + norm_back(grad, xhat, inv, gain2)
        gtwo[span, :] = total
        low[span, :] = total.astype(bf16)
        return 0

    lax.fori_loop(0, rows // SEQ, top, 0)
    gmix[...] = mm_nt(low[...], w_cross[...]).astype(bf16)
    grad_cross = mm_tn(mix[...], low[...]).astype(bf16)
    scaled = lane_masks(SCALE)
    plain = lane_masks(1.0)

    def attend(p, _):
        span = pl.ds(pl.multiple_of(p * 2 * SEQ, 2 * SEQ), 2 * SEQ)
        toks = pl.ds(pl.multiple_of(p * IMG_TOK, IMG_TOK), IMG_TOK)
        for h in range(PAIRS):
            at = 2 * HEAD_DIM * h
            q = two_heads(cq[span, at : at + 128], scaled)
            gm = two_heads(gmix[span, at : at + 128], plain)
            k = kv[toks, at : at + 128]
            v = kv[toks, D + at : D + at + 128]
            pl_ = probs[p, h]
            pf = pl_.astype(f32)
            gp = mm_nt(gm, v)
            delta = jnp.sum(pf * gp, axis=-1, keepdims=True)
            gs = (pf * (gp - delta)).astype(bf16)
            gcq[span, at : at + 128] = (join_heads(mm(gs, k), 2 * SEQ) * SCALE).astype(bf16)
            gkv[toks, at : at + 128] = mm_tn(gs, q).astype(bf16)
            gkv[toks, D + at : D + at + 128] = mm_tn(pl_, gm).astype(bf16)
        return 0

    lax.fori_loop(0, images, attend, 0)
    grad_query = mm_tn(cin[...], gcq[...]).astype(bf16)
    for j in range(2):
        cols = slice(j * D, (j + 1) * D)
        grad_kv = mm_tn(tokens[...], gkv[:, cols]).astype(bf16)

        def first(ref):
            if j == 0:
                store_blocks(ref, flip, slice(0, D), grad_cross)
                store_blocks(ref, flip, slice(D, 2 * D), grad_query)

        def second(ref):
            store_blocks(ref, flip, cols, grad_kv)

        store_split(core, keep, send, first, second)
    gimg_out[...] = mm_nt(gkv[...], w_kv[...])
    gone_out[...] = mm_nt(gcq[...], w_query[...])

    def bottom(i, _):
        span = pl.ds(pl.multiple_of(i * SEQ, SEQ), SEQ)
        grad = gone_out[span, :]
        xhat, inv = normed(one[span, :])
        small_out[2:3, :] += jnp.sum(grad * xhat, axis=0, keepdims=True)
        small_out[3:4, :] += jnp.sum(grad, axis=0, keepdims=True)
        gone_out[span, :] = gtwo[span, :] + norm_back(grad, xhat, inv, gain1)
        return 0

    lax.fori_loop(0, rows // SEQ, bottom, 0)


def cross_back(plan, acc, gn, two, one, g, gain, b_out, w_cross, w_query, w_kv, mix, probs, kv, cq, cin, tokens):
    rows = cq.shape[0]
    toks = tokens.shape[0]
    return pl.pallas_call(
        cross_back_kernel,
        out_shape=[
            sds((rows // SEQ, SEQ, D), bf16),
            sds((BLOCKS, BLOCK, WIDE_COLS), bf16),
            sds((BLOCKS, BLOCK, WIDE_COLS), bf16),
            sds((rows, D), f32),
            sds((toks, D), f32),
            sds((8, D), f32),
        ],
        in_specs=[SM] + [VM] * 16,
        out_specs=[VM] * 6,
        scratch_shapes=[
            pltpu.VMEM((rows, D), f32),
            pltpu.VMEM((rows, D), bf16),
            pltpu.VMEM((rows, D), bf16),
            pltpu.VMEM((rows, D), bf16),
            pltpu.VMEM((toks, 2 * D), bf16),
        ],
        compiler_params=params(),
        cost_estimate=cost(rows * D * D * 20 * 2, 30e6),
        name="cross_back",
    )(plan, acc, gn, two, one, g, gain, b_out.reshape(1, D), w_cross, w_query, w_kv, mix, probs, kv, cq, cin, tokens)


def self_back_kernel(
    plan, gone, x, attn, qkv, probs, mix, gain, w_self, w_qkv,
    hid_out, keep, send, small_out, low, gmix, gqkv, gbase,
):
    rows = x.shape[0]
    flip = plan[FLIP]
    core = plan[CORE]
    gain0 = gain[0:1, :].astype(f32)
    small_out[...] = jnp.zeros_like(small_out)
    low[...] = gone[...].astype(bf16)
    gmix[...] = mm_nt(low[...], w_self[...]).astype(bf16)
    grad_self = mm_tn(mix[...], low[...]).astype(bf16)
    scaled = lane_masks(SCALE)
    plain = lane_masks(1.0)

    def attend(p, _):
        span = pl.ds(pl.multiple_of(p * 2 * SEQ, 2 * SEQ), 2 * SEQ)
        for h in range(PAIRS):
            at = 2 * HEAD_DIM * h
            q = two_heads(qkv[span, at : at + 128], scaled)
            gm = two_heads(gmix[span, at : at + 128], plain)
            k = qkv[span, D + at : D + at + 128]
            v = qkv[span, 2 * D + at : 2 * D + at + 128]
            pl_ = probs[p, h]
            pf = pl_.astype(f32)
            gp = mm_nt(gm, v)
            delta = jnp.sum(pf * gp, axis=-1, keepdims=True)
            gs = (pf * (gp - delta)).astype(bf16)
            gqkv[span, at : at + 128] = (join_heads(mm(gs, k), 2 * SEQ) * SCALE).astype(bf16)
            gqkv[span, D + at : D + at + 128] = mm_tn(gs, q).astype(bf16)
            gqkv[span, 2 * D + at : 2 * D + at + 128] = mm_tn(pl_, gm).astype(bf16)
        return 0

    lax.fori_loop(0, rows // (2 * SEQ), attend, 0)
    for j in range(3):
        grad = mm_tn(attn[...], gqkv[:, j * D : (j + 1) * D]).astype(bf16)

        def first(ref):
            if j == 0:
                store_blocks(ref, flip, slice(0, D), grad_self)
                store_blocks(ref, flip, slice(D, 2 * D), grad)

        def second(ref):
            if j > 0:
                store_blocks(ref, flip, slice((j - 1) * D, j * D), grad)

        store_split(core, keep, send, first, second)
    gbase[...] = mm_nt(gqkv[...], w_qkv[...])

    def bottom(i, _):
        span = pl.ds(pl.multiple_of(i * SEQ, SEQ), SEQ)
        grad = gbase[span, :]
        xhat, inv = normed(x[span, :].astype(f32))
        small_out[0:1, :] += jnp.sum(grad * xhat, axis=0, keepdims=True)
        small_out[1:2, :] += jnp.sum(grad, axis=0, keepdims=True)
        hid_out[i] = gone[span, :] + norm_back(grad, xhat, inv, gain0)
        return 0

    lax.fori_loop(0, rows // SEQ, bottom, 0)


def self_back(plan, gone, x, attn, qkv, probs, mix, gain, w_self, w_qkv):
    rows = x.shape[0]
    return pl.pallas_call(
        self_back_kernel,
        out_shape=[
            sds((rows // SEQ, SEQ, D), f32),
            sds((BLOCKS, BLOCK, WIDE_COLS), bf16),
            sds((BLOCKS, BLOCK, WIDE_COLS), bf16),
            sds((8, D), f32),
        ],
        in_specs=[SM] + [VM] * 9,
        out_specs=[VM] * 4,
        scratch_shapes=[
            pltpu.VMEM((rows, D), bf16),
            pltpu.VMEM((rows, D), bf16),
            pltpu.VMEM((rows, 3 * D), bf16),
            pltpu.VMEM((rows, D), f32),
        ],
        compiler_params=params(),
        cost_estimate=cost(rows * D * D * 16 * 2, 25e6),
        name="self_back",
    )(plan, gone, x, attn, qkv, probs, mix, gain, w_self, w_qkv)


def swap(value, axis, bit):
    size = lax.axis_size(axis)
    return lax.ppermute(value, axis, [(i, i ^ bit) for i in range(size)])


def add(a, b):
    return (a.astype(f32) + b.astype(f32)).astype(bf16)


STEPS = (("narrow", 1), ("wide", 2), ("wide", 4), ("wide", 8))


def reduce_chunk(keep, send):
    got = swap(send, "wide", 1)
    for axis, bit in STEPS:
        half = keep.shape[0] // 2
        out = add(keep[half:], got[half:])
        keep = add(keep[:half], got[:half])
        got = swap(out, axis, bit)
    piece = add(keep, got)
    for axis, bit in STEPS[:0:-1]:
        piece = jnp.concatenate([piece, swap(piece, axis, bit)])
    return piece, swap(piece, "wide", 1)


def load_piece(plan, mine, theirs, half, index, store):
    slot = index ^ (plan[FLIP] % 8)
    core = plan[CORE]

    @pl.when(core == half)
    def _():
        store(mine[slot].astype(f32))

    @pl.when(core != half)
    def _():
        store(theirs[slot].astype(f32))


def finish_columns_kernel(cuts, plan, mine, theirs, *outs):
    for w in range(8):
        for half in range(2):

            def store(value, half=half, w=w):
                for number, src, dst, width in cuts[half]:
                    outs[number][w * BLOCK : (w + 1) * BLOCK, dst : dst + width] = value[:, src : src + width]

            load_piece(plan, mine, theirs, half, w, store)


def finish_columns(plan, pieces, cuts, widths, name):
    return pl.pallas_call(
        functools.partial(finish_columns_kernel, cuts),
        out_shape=[sds((8 * BLOCK, width), f32) for width in widths],
        in_specs=[SM, VM, VM],
        out_specs=[VM] * len(widths),
        compiler_params=params(24),
        cost_estimate=cost(0, 8e6),
        name=name,
    )(plan, *pieces)


def finish_mlp_kernel(plan, mine_a, theirs_a, mine_b, theirs_b, grad_in, grad_out):
    for call, mine, theirs in ((0, mine_a, theirs_a), (1, mine_b, theirs_b)):
        for w in range(8):

            def first(value, w=w, call=call):
                rows = slice(w * BLOCK, (w + 1) * BLOCK)
                for n in range(2):
                    dst = n * 6 * TILE + call * 3 * TILE
                    grad_in[rows, dst : dst + 3 * TILE] = value[:, n * D : (n + 1) * D]

            def second(value, w=w, call=call):
                for j in range(3):
                    for half in range(2):
                        dst = (3 * call + j) * TILE + w * 32 + half * 16
                        grad_out[dst : dst + 16, :] = value[j * 16 : (j + 1) * 16, half * D : (half + 1) * D]

            load_piece(plan, mine, theirs, 0, w, first)
            load_piece(plan, mine, theirs, 1, w, second)


def finish_mlp(plan, a, b):
    return pl.pallas_call(
        finish_mlp_kernel,
        out_shape=[sds((8 * BLOCK, FF), f32), sds((FF // 2, D), f32)],
        in_specs=[SM] + [VM] * 4,
        out_specs=[VM] * 2,
        compiler_params=params(40),
        cost_estimate=cost(0, 16e6),
        name="finish_mlp",
    )(plan, *a, *b)


def plain_sum(value):
    shard = lax.psum_scatter(value, "narrow", scatter_dimension=0, tiled=True)
    return lax.psum(shard, "wide").astype(f32)


def plain_sums(core, chunks):
    whole = []
    for keep, send in chunks:
        first = jnp.where(core == 0, keep, send)
        second = jnp.where(core == 0, send, keep)
        whole.append((first.reshape(D, WIDE_COLS), second))
    grad_in = jnp.stack([whole[0][0].reshape(D, 2, 3 * TILE), whole[1][0].reshape(D, 2, 3 * TILE)], axis=2)
    grad_out = jnp.stack([whole[0][1], whole[1][1]]).reshape(2, 2, 8, 3, 16, 2, D)
    grad_out = grad_out.transpose(1, 0, 3, 2, 5, 4, 6).reshape(FF, D)
    crosses, keys = whole[2][0], whole[2][1].reshape(D, WIDE_COLS)
    front_half, back_half = whole[3][0], whole[3][1].reshape(D, WIDE_COLS)
    return [
        plain_sum(v)
        for v in (
            jnp.concatenate([front_half[:, D:], back_half], axis=1),
            front_half[:, :D],
            crosses[:, D:],
            keys,
            crosses[:, :D],
            grad_in.reshape(D, FF),
            grad_out,
        )
    ]


def local(
    hidden_in, image_tokens, image_group, caption_len, norm_gain, norm_bias, self_qkv, self_out, cross_query,
    cross_kv, cross_out, mlp_in, mlp_bias_in, mlp_out, mlp_bias_out, out_grad,
):
    narrow = lax.axis_size("narrow")
    wide = lax.axis_size("wide")
    images, toks, _ = image_tokens.shape
    mine = images // narrow
    caps = 2 * mine
    rows = caps * SEQ
    n_at, w_at = lax.axis_index("narrow"), lax.axis_index("wide")
    fast = narrow == 2 and wide == 16
    core = w_at % 2
    if fast:
        flip = n_at * 8 + (w_at // 2) % 2 * 4 + (w_at // 4) % 2 * 2 + (w_at // 8) % 2
    else:
        flip = jnp.zeros_like(n_at)
    pos = jnp.stack([n_at, w_at * images, flip, core]).astype(jnp.int32)
    plan = make_plan(narrow, images, image_group, caption_len, pos)
    if narrow == 2:
        own, away = pick_tokens(plan, image_tokens, mine)
        got = swap(away, "narrow", 1)
        tokens = jnp.concatenate([own, got], axis=1).reshape(mine * IMG_TOK, D)
    else:
        every = lax.all_gather(image_tokens, "narrow")
        first = n_at * mine
        tokens = lax.dynamic_slice_in_dim(every, first, mine, 1).transpose(1, 0, 2, 3)
        tokens = tokens.reshape(mine * IMG_TOK, D)
    x, g, attn, qkv, self_probs, self_mix, one, cin, cq = front(
        rows, plan, hidden_in, out_grad, norm_gain, norm_bias, self_qkv, self_out, cross_query
    )
    kv, cross_probs, cross_mix, two, min_ = cross(tokens, cq, one, norm_gain, norm_bias, cross_kv, cross_out)
    zero = jnp.zeros((rows, D), f32)
    acc, gn, keep0, send0, gbias0 = mlp(0, plan, min_, g, zero, zero, mlp_in, mlp_bias_in, mlp_out)
    acc, gn, keep1, send1, gbias1 = mlp(1, plan, min_, g, acc, gn, mlp_in, mlp_bias_in, mlp_out)
    hidden_out, keep2, send2, gone, gimg, small2 = cross_back(
        plan, acc, gn, two, one, g, norm_gain, mlp_bias_out, cross_out, cross_query, cross_kv, cross_mix,
        cross_probs, kv, cq, cin, tokens,
    )
    grad_hidden, keep3, send3, small3 = self_back(
        plan, gone, x, attn, qkv, self_probs, self_mix, norm_gain, self_out, self_qkv
    )
    chunks = ((keep0, send0), (keep1, send1), (keep2, send2), (keep3, send3))
    if fast:
        parts = [reduce_chunk(keep, send) for keep, send in chunks]
        grad_mlp_in, grad_mlp_out = finish_mlp(plan, parts[0], parts[1])
        grad_cross_out, grad_query, grad_kv = finish_columns(
            plan, parts[2], (((0, 0, 0, D), (1, D, 0, D)), ((2, 0, 0, 2 * D),)), (D, D, 2 * D), "finish_cross"
        )
        grad_self_out, grad_qkv = finish_columns(
            plan, parts[3], (((0, 0, 0, D), (1, D, 0, D)), ((1, 0, D, 2 * D),)), (D, 3 * D), "finish_self"
        )
    else:
        grad_qkv, grad_self_out, grad_query, grad_kv, grad_cross_out, grad_mlp_in, grad_mlp_out = plain_sums(
            core, chunks
        )
    bias_in = jnp.stack([gbias0.reshape(2, 3 * TILE), gbias1.reshape(2, 3 * TILE)], axis=1).reshape(4, D)
    small = jnp.concatenate([small3[0:1], small2[2:3], small2[0:1], small3[1:2], small2[3:4], small2[1:2], small2[4:5], bias_in])
    small = lax.psum(small, ("wide", "narrow"))
    share = D // narrow
    columns = lax.dynamic_slice_in_dim(small[:7], n_at * share, share, 1)
    grad_bias_in = lax.dynamic_slice_in_dim(small[7:].reshape(FF), n_at * (FF // narrow), FF // narrow, 0)
    gimg = gimg.reshape(mine, IMG_TOK, D)
    if narrow == 2:
        hid_got = swap(hidden_out.reshape(mine, 2, SEQ, D)[:, 1], "narrow", 1)
        grad_got = swap(grad_hidden.reshape(mine, 2, SEQ, D)[:, 1].astype(bf16), "narrow", 1)
        img_got = swap(gimg[:, toks:].astype(bf16), "narrow", 1)
        final_out = place(OUT_SRC, caps, plan, hidden_out, hid_got, bf16, "place_out")
        final_grad = place(OUT_SRC, caps, plan, grad_hidden, grad_got, f32, "place_grad")
        grad_image = place(IMG_SRC, images, plan, gimg[:, :toks], img_got, f32, "place_image")
    else:
        out_all = lax.all_gather(hidden_out, "narrow", tiled=True)
        grad_all = lax.all_gather(grad_hidden.astype(bf16), "narrow", tiled=True)
        final_out = place(OUT_SRC, caps, plan, out_all, out_all[:1], bf16, "place_out")
        final_grad = place(OUT_SRC, caps, plan, grad_all, grad_all[:1], f32, "place_grad")
        every = lax.all_gather(gimg.astype(bf16), "narrow", tiled=True)
        grad_image = lax.dynamic_slice_in_dim(every, n_at * toks, toks, 1).astype(f32)
    return (
        final_out.reshape(rows, D),
        final_grad.reshape(rows, D),
        grad_image,
        columns[:3],
        columns[3:6],
        grad_qkv,
        grad_self_out,
        grad_query,
        grad_kv,
        grad_cross_out,
        grad_mlp_in,
        grad_bias_in,
        grad_mlp_out,
        columns[6],
    )


def solution(mesh):
    in_specs = (
        P("wide", None),
        P("wide", "narrow", None),
        P("wide"),
        P("wide"),
    ) + (P(),) * 11 + (P("wide", None),)
    out_specs = (
        P(("wide", "narrow"), None),
        P(("wide", "narrow"), None),
        P("wide", "narrow", None),
        P(None, "narrow"),
        P(None, "narrow"),
        P("narrow", None),
        P("narrow", None),
        P("narrow", None),
        P("narrow", None),
        P("narrow", None),
        P("narrow", None),
        P("narrow"),
        P("narrow", None),
        P("narrow"),
    )
    return jax.shard_map(local, mesh=mesh, in_specs=in_specs, out_specs=out_specs, check_vma=False)
```

```python
import functools

import jax
import jax.numpy as jnp
from jax import lax
from jax.experimental import pallas as pl
from jax.experimental.pallas import tpu as pltpu
from jax.sharding import PartitionSpec as P

D = 768
HEADS = 12
HEAD_DIM = 64
FF = 3072
SEQ = 64
IMG_TOK = 256
PAIRS = HEADS // 2
SCALE = HEAD_DIM**-0.5
BLOCK = 48
BLOCKS = D // BLOCK
WIDE_COLS = 2 * D
TILE = 256
f32 = jnp.float32
bf16 = jnp.bfloat16
VM = pl.BlockSpec(memory_space=pltpu.VMEM)
SM = pl.BlockSpec(memory_space=pltpu.SMEM)
ANY = pl.BlockSpec(memory_space=pl.ANY)
CORE_PARTS = 4
CAPS, LENS, MINE, PEER, IMG_SRC, OUT_SRC, FLIP, CORE, PLAN = 0, 8, 16, 20, 24, 32, 40, 41, 48


def mm(left, right):
    return lax.dot_general(left, right, (((1,), (0,)), ((), ())), preferred_element_type=f32)


def mm_nt(left, right):
    return lax.dot_general(left, right, (((1,), (1,)), ((), ())), preferred_element_type=f32)


def mm_tn(left, right):
    return lax.dot_general(left, right, (((0,), (0,)), ((), ())), preferred_element_type=f32)


def params(vmem=56, grid=None):
    return pltpu.CompilerParams(
        vmem_limit_bytes=vmem * 1024 * 1024,
        dimension_semantics=None if grid is None else ("arbitrary",) * grid,
    )


def cost(*_):
    return pl.CostEstimate(flops=1024, bytes_accessed=1024, transcendentals=0)


def sds(shape, dtype):
    return jax.ShapeDtypeStruct(shape, dtype)


def normed(x):
    center = x - jnp.mean(x, axis=-1, keepdims=True)
    inv = lax.rsqrt(jnp.mean(center * center, axis=-1, keepdims=True) + 1e-05)
    return center * inv, inv


def norm_back(grad, xhat, inv, gain):
    u = grad * gain
    return inv * (
        u - jnp.mean(u, axis=-1, keepdims=True) - xhat * jnp.mean(u * xhat, axis=-1, keepdims=True)
    )


def lane_masks(scale):
    lane = lax.broadcasted_iota(jnp.int32, (1, 2 * HEAD_DIM), 1)
    low = jnp.where(lane < HEAD_DIM, scale, 0.0).astype(bf16)
    high = jnp.where(lane < HEAD_DIM, 0.0, scale).astype(bf16)
    return low, high


def two_heads(x, masks):
    return jnp.concatenate([x * masks[0], x * masks[1]], axis=0)


def join_heads(x, rows):
    lane = lax.broadcasted_iota(jnp.int32, (rows, 2 * HEAD_DIM), 1)
    return jnp.where(lane < HEAD_DIM, x[:rows], x[rows:])


def plan_kernel(narrow, images, group, lens, pos, out, place, count):
    me = pos[0]
    base = pos[1]
    half = images // narrow
    caps = 2 * images
    for p in range(images):
        count[p] = 0
    for c in range(caps):
        g = group[c] - base
        n = count[g]
        place[2 * g + n] = c
        count[g] = n + 1
    for i in range(PLAN):
        out[i] = 0
    out[FLIP] = pos[2]
    out[CORE] = pos[3]
    slots = [jnp.int32(0) for _ in range(2)]
    turn = jnp.int32(0)
    for p in range(images):
        a = place[2 * p]
        b = place[2 * p + 1]
        if narrow == 2:
            both_low = b < images
            both_high = a >= images
            mixed = jnp.logical_not(jnp.logical_or(both_low, both_high))
            owner = jnp.where(both_low, 0, jnp.where(both_high, 1, turn))
            turn = jnp.where(mixed, 1 - turn, turn)
            slot = jnp.where(owner == 0, slots[0], slots[1])
            slots[0] = jnp.where(owner == 0, slots[0] + 1, slots[0])
            slots[1] = jnp.where(owner == 1, slots[1] + 1, slots[1])
            swap = jnp.logical_and(mixed, owner == 1)
            first = jnp.where(swap, b, a)
            second = jnp.where(swap, a, b)
            mine = owner == me

            @pl.when(mine)
            def _():
                out[MINE + slot] = p
                out[CAPS + 2 * slot] = first
                out[CAPS + 2 * slot + 1] = second
                out[LENS + 2 * slot] = lens[first]
                out[LENS + 2 * slot + 1] = lens[second]

            @pl.when(jnp.logical_not(mine))
            def _():
                out[PEER + slot] = p

            out[IMG_SRC + p] = jnp.where(mine, slot, half + slot)
            for k, c in ((0, first), (1, second)):

                @pl.when(c // images == me)
                def _():
                    out[OUT_SRC + c - me * images] = jnp.where(mine, 2 * slot + k, caps // 2 + slot)

        else:
            owner = p // half
            slot = p % half
            mine = owner == me
            per = caps // narrow

            @pl.when(mine)
            def _():
                out[MINE + slot] = p
                for k, c in ((0, a), (1, b)):
                    out[CAPS + 2 * slot + k] = c
                    out[LENS + 2 * slot + k] = lens[c]

            for k, c in ((0, a), (1, b)):

                @pl.when(c // per == me)
                def _():
                    out[OUT_SRC + c - me * per] = 2 * p + k


def make_plan(narrow, images, group, lens, pos):
    return pl.pallas_call(
        functools.partial(plan_kernel, narrow, images),
        out_shape=sds((PLAN,), jnp.int32),
        in_specs=[SM, SM, SM],
        out_specs=SM,
        scratch_shapes=[
            pltpu.SMEM((2 * images,), jnp.int32),
            pltpu.SMEM((images,), jnp.int32),
        ],
        compiler_params=params(4),
        name="plan",
    )(group, lens, pos)


def pick_kernel(plan, tokens_a, tokens_b, mine, peer):
    mine[...] = tokens_a[...]
    peer[...] = tokens_b[...]


def pick_tokens(plan, tokens, count):
    block = (1,) + tokens.shape[1:]
    return pl.pallas_call(
        pick_kernel,
        grid_spec=pltpu.PrefetchScalarGridSpec(
            num_scalar_prefetch=1,
            grid=(count,),
            in_specs=[
                pl.BlockSpec(block, lambda i, plan: (plan[MINE + i], 0, 0)),
                pl.BlockSpec(block, lambda i, plan: (plan[PEER + i], 0, 0)),
            ],
            out_specs=[pl.BlockSpec(block, lambda i, plan: (i, 0, 0))] * 2,
        ),
        out_shape=[sds((count,) + tokens.shape[1:], bf16)] * 2,
        compiler_params=params(8),
        name="pick",
    )(plan, tokens, tokens)


def place_kernel(offset, count, plan, own, got, out):
    have = own.shape[0]
    for i in range(count):
        src = plan[offset + i]

        @pl.when(src < have)
        def _():
            out[i] = own[jnp.minimum(src, have - 1)].astype(out.dtype)

        @pl.when(src >= have)
        def _():
            out[i] = got[jnp.maximum(src - have, 0)].astype(out.dtype)


def place(offset, count, plan, own, got, dtype, name):
    return pl.pallas_call(
        functools.partial(place_kernel, offset, count),
        out_shape=sds((count,) + own.shape[1:], dtype),
        in_specs=[SM, VM, VM],
        out_specs=VM,
        compiler_params=params(24),
        cost_estimate=cost(0, 4 * count * own.shape[1] * own.shape[2] * 2),
        name=name,
    )(plan, own, got)


WINDOW = 4


def staged(name, body, smem, ins, outs, extra=(), late=(), chunk=False):
    n_s, n_i, n_o, n_e = len(smem), len(ins), len(outs), len(extra)
    n_c = 1 + CORE_PARTS if chunk else 0
    staged_ins = [i for i in range(n_i) if i not in late]

    def kernel(*refs):
        refs = list(refs)
        take = lambda n: [refs.pop(0) for _ in range(n)]
        scalars, h_in, h_out = take(n_s), take(n_i), take(n_o)
        chunk_out = take(n_c)
        v_in = dict(zip(staged_ins, take(len(staged_ins))))
        v_out, more = take(n_o), take(n_e)
        staging = Staging(chunk_out, *take(3)) if chunk else None
        in_sem, out_sem = refs
        copies = {i: pltpu.make_async_copy(h_in[i], v_in[i], in_sem.at[i]) for i in staged_ins}
        started, waited, going = [], set(), []

        def ahead(count):
            for i in staged_ins:
                if count <= 0:
                    return
                if i not in started:
                    copies[i].start()
                    started.append(i)
                    count -= 1

        ahead(WINDOW)

        def load(i):
            if i in late:
                return h_in[i]
            if i not in waited:
                assert i in started
                copies[i].wait()
                waited.add(i)
                ahead(1)
            return v_in[i]

        def send(i):
            copy = pltpu.make_async_copy(v_out[i], h_out[i], out_sem.at[i])
            copy.start()
            going.append((i, copy))

        body(scalars, load, v_out, send, more, *([staging] if chunk else []))
        sent = {i for i, _ in going}
        for i in range(n_o):
            if i not in sent and outs[i] is not None:
                send(i)
        for i in staged_ins:
            load(i)
        for _, copy in going:
            copy.wait()
        if chunk:
            staging.wait()

    return pl.pallas_call(
        kernel,
        out_shape=[sds(*o) for o in outs] + [sds(*o) for o in CHUNK_OUTS[:n_c]],
        in_specs=[SM] * n_s + [ANY] * n_i,
        out_specs=[ANY] * (n_o + n_c),
        scratch_shapes=[pltpu.VMEM(ins[i].shape, ins[i].dtype) for i in staged_ins]
        + [pltpu.VMEM(*o) for o in outs]
        + list(extra)
        + (chunk_extra() if chunk else [])
        + [pltpu.SemaphoreType.DMA((max(n_i, 1),)), pltpu.SemaphoreType.DMA((max(n_o, 1),))],
        compiler_params=params(),
        cost_estimate=cost(),
        name=name,
    )(*smem, *ins)


def unrolled(count, step):
    for i in range(count):
        step(i)


def front(rows, plan, hidden, out_grad, gain, bias, w_qkv, w_self, w_query, own, w_kv):
    pairs = rows // (2 * SEQ)
    kv_rows = 0 if own is None else own.shape[0]

    def body(smem, load, out, send, extra):
        (plan,) = smem
        x_out, attn_out, qkv_out, probs_out, mix_out, one_out, cin_out, cq_out, kv_out = out
        hidden = load(0)
        gain, bias = load(1), load(2)
        gain0, bias0 = gain[0:1, :].astype(f32), bias[0:1, :].astype(f32)
        gain1, bias1 = gain[1:2, :].astype(f32), bias[1:2, :].astype(f32)

        def gather(i):
            src = pl.ds(pl.multiple_of(plan[CAPS + i] * SEQ, SEQ), SEQ)
            dst = slice(i * SEQ, (i + 1) * SEQ)
            x = hidden[src, :]
            x_out[dst, :] = x
            attn_out[dst, :] = (normed(x.astype(f32))[0] * gain0 + bias0).astype(bf16)

        unrolled(rows // SEQ, gather)
        send(0)
        send(1)
        w_qkv = load(3)
        for j in range(3):
            cols = slice(j * D, (j + 1) * D)
            qkv_out[:, cols] = mm(attn_out[...], w_qkv[:, cols]).astype(bf16)
        send(2)
        masks = lane_masks(SCALE)
        row = lax.broadcasted_iota(jnp.int32, (2 * SEQ, 2 * SEQ), 0)
        col = lax.broadcasted_iota(jnp.int32, (2 * SEQ, 2 * SEQ), 1)
        causal = jnp.logical_and(col <= row, (col // SEQ) == (row // SEQ))

        def attend(p):
            span = slice(p * 2 * SEQ, (p + 1) * 2 * SEQ)
            length = jnp.where(col < SEQ, plan[LENS + 2 * p], plan[LENS + 2 * p + 1])
            allowed = jnp.logical_and(causal, (col % SEQ) < length)
            fill = jnp.where(allowed, 0.0, -1e30)
            fill = jnp.concatenate([fill, fill], axis=0)
            for h in range(PAIRS):
                at = 2 * HEAD_DIM * h
                q = two_heads(qkv_out[span, at : at + 128], masks)
                k = qkv_out[span, D + at : D + at + 128]
                v = qkv_out[span, 2 * D + at : 2 * D + at + 128]
                logits = jnp.where(fill < 0.0, fill, mm_nt(q, k))
                e = jnp.exp(logits - jnp.max(logits, axis=-1, keepdims=True))
                low = (e * (1.0 / jnp.sum(e, axis=-1, keepdims=True))).astype(bf16)
                probs_out[p, h] = low
                mix_out[span, at : at + 128] = join_heads(mm(low, v), 2 * SEQ).astype(bf16)

        unrolled(pairs, attend)
        send(3)
        send(4)
        one_out[...] = mm(mix_out[...], load(4)[...])

        def second(i):
            span = slice(i * SEQ, (i + 1) * SEQ)
            one = one_out[span, :] + x_out[span, :].astype(f32)
            one_out[span, :] = one
            cin_out[span, :] = (normed(one)[0] * gain1 + bias1).astype(bf16)

        unrolled(rows // SEQ, second)
        send(5)
        send(6)
        cq_out[...] = mm(cin_out[...], load(5)[...]).astype(bf16)
        send(7)
        if own is not None:
            for j in range(2):
                cols = slice(j * D, (j + 1) * D)
                kv_out[:, cols] = mm(load(6)[...], load(7)[:, cols]).astype(bf16)

    ins = [hidden, gain, bias, w_qkv, w_self, w_query] + ([] if own is None else [own, w_kv])
    return staged(
        "front",
        body,
        [plan],
        ins,
        [
            ((rows, D), bf16),
            ((rows, D), bf16),
            ((rows, 3 * D), bf16),
            ((pairs, PAIRS, 4 * SEQ, 2 * SEQ), bf16),
            ((rows, D), bf16),
            ((rows, D), f32),
            ((rows, D), bf16),
            ((rows, D), bf16),
            ((max(kv_rows, 16), 2 * D), bf16),
        ],
    )


def cross(plan, kv_own, tokens, cq, one, gain, bias, w_kv, w_cross, out_grad):
    rows = cq.shape[0]
    images = rows // (2 * SEQ)
    each = tokens.shape[0] // images
    has = IMG_TOK - each

    def body(smem, load, out, send, extra):
        (plan,) = smem
        kv_out, probs_out, mix_out, two_out, min_out, g_out = out
        raw, grads_in = extra
        gather = [
            pltpu.make_async_copy(
                load(8).at[pl.ds(pl.multiple_of(plan[CAPS + i] * SEQ, SEQ), SEQ), :],
                g_out.at[pl.ds(i * SEQ, SEQ), :],
                grads_in.at[i],
            )
            for i in range(rows // SEQ)
        ]
        for copy in gather:
            copy.start()
        tokens, w_kv = load(0), load(1)
        for j in range(2):
            cols = slice(j * D, (j + 1) * D)
            raw[:, cols] = mm(tokens[...], w_kv[:, cols]).astype(bf16)
        for p in range(images):
            kv_out[p * IMG_TOK + has : (p + 1) * IMG_TOK, :] = raw[p * each : (p + 1) * each, :]
            if has:
                kv_out[p * IMG_TOK : p * IMG_TOK + has, :] = load(2)[p * has : (p + 1) * has, :]
        send(0)
        cq = load(3)
        masks = lane_masks(SCALE)

        def attend(p):
            span = slice(p * 2 * SEQ, (p + 1) * 2 * SEQ)
            toks = slice(p * IMG_TOK, (p + 1) * IMG_TOK)
            for h in range(PAIRS):
                at = 2 * HEAD_DIM * h
                q = two_heads(cq[span, at : at + 128], masks)
                logits = mm_nt(q, kv_out[toks, at : at + 128])
                e = jnp.exp(logits - jnp.max(logits, axis=-1, keepdims=True))
                low = (e * (1.0 / jnp.sum(e, axis=-1, keepdims=True))).astype(bf16)
                probs_out[p, h] = low
                mix = mm(low, kv_out[toks, D + at : D + at + 128])
                mix_out[span, at : at + 128] = join_heads(mix, 2 * SEQ).astype(bf16)

        unrolled(images, attend)
        send(1)
        send(2)
        two_out[...] = mm(mix_out[...], load(4)[...])
        one, gain, bias = load(5), load(6), load(7)
        gain2, bias2 = gain[2:3, :].astype(f32), bias[2:3, :].astype(f32)

        def second(i):
            span = slice(i * SEQ, (i + 1) * SEQ)
            two = two_out[span, :] + one[span, :]
            two_out[span, :] = two
            min_out[span, :] = (normed(two)[0] * gain2 + bias2).astype(bf16)

        unrolled(rows // SEQ, second)
        for copy in gather:
            copy.wait()

    return staged(
        "cross",
        body,
        [plan],
        [tokens, w_kv, kv_own, cq, w_cross, one, gain, bias, out_grad],
        [
            ((images * IMG_TOK, 2 * D), bf16),
            ((images, PAIRS, 4 * SEQ, IMG_TOK), bf16),
            ((rows, D), bf16),
            ((rows, D), f32),
            ((rows, D), bf16),
            ((rows, D), bf16),
        ],
        [pltpu.VMEM((tokens.shape[0], 2 * D), bf16), pltpu.SemaphoreType.DMA((rows // SEQ,))],
        late=(8,),
    )


CHUNK_OUTS = [((BLOCKS, BLOCK, WIDE_COLS), bf16)] + [((BLOCKS // CORE_PARTS, BLOCK, WIDE_COLS), bf16)] * CORE_PARTS


def chunk_extra():
    return [
        pltpu.VMEM((BLOCKS, BLOCK, WIDE_COLS), bf16),
        pltpu.VMEM((BLOCKS, BLOCK, WIDE_COLS), bf16),
        pltpu.SemaphoreType.DMA((1 + CORE_PARTS,)),
    ]


class Staging:
    def __init__(self, outs, first, second, sems):
        self.keep, *self.parts = outs
        self.first, self.second, self.sems = first, second, sems

    def copies(self, kept, sent):
        size = BLOCKS // CORE_PARTS
        return [pltpu.make_async_copy(kept, self.keep, self.sems.at[CORE_PARTS])] + [
            pltpu.make_async_copy(sent.at[pl.ds(i * size, size)], self.parts[i], self.sems.at[i])
            for i in range(CORE_PARTS)
        ]

    def send(self, core):
        @pl.when(core == 0)
        def _():
            for copy in self.copies(self.first, self.second):
                copy.start()

        @pl.when(core != 0)
        def _():
            for copy in self.copies(self.second, self.first):
                copy.start()

    def wait(self):
        for copy in self.copies(self.first, self.second):
            copy.wait()


def store_blocks(ref, flip, cols, value):
    for b in range(BLOCKS):
        ref[b ^ flip, :, cols] = value[b * BLOCK : (b + 1) * BLOCK, :]


def mlp(call, plan, min_, g, acc, gn, w_in, b_in, w_out):
    rows = g.shape[0]
    tiles = [k + 3 * (k // 3) + 3 * call for k in range(6)]
    carried = acc is not None

    def kernel(*refs):
        refs = list(refs)
        take = lambda n: [refs.pop(0) for _ in range(n)]
        (plan,) = take(1)
        h_min, h_g, h_bias, h_in, h_out = take(5)
        h_acc, h_gn = take(2) if carried else (None, None)
        o_acc, o_gn, o_bias, o_keep = take(4)
        o_parts = take(CORE_PARTS)
        v_min, v_g, v_bias, v_in, v_out, v_acc, v_gn, gbias, act, low, min_t, first, second, chunk_sem, sems = refs
        flip = plan[FLIP]
        staging = Staging([o_keep] + o_parts, first, second, chunk_sem)
        copies = [
            pltpu.make_async_copy(h_min, v_min, sems.at[0]),
            pltpu.make_async_copy(h_bias, v_bias, sems.at[1]),
        ]
        for k, t in enumerate(tiles):
            mine, there = pl.ds(k * TILE, TILE), pl.ds(t * TILE, TILE)
            copies.append(pltpu.make_async_copy(h_in.at[:, there], v_in.at[:, mine], sems.at[2 + 2 * k]))
            copies.append(pltpu.make_async_copy(h_out.at[there, :], v_out.at[mine, :], sems.at[3 + 2 * k]))
        copies.insert(3, pltpu.make_async_copy(h_g, v_g, sems.at[14]))
        if carried:
            copies.append(pltpu.make_async_copy(h_acc, v_acc, sems.at[15]))
            copies.append(pltpu.make_async_copy(h_gn, v_gn, sems.at[16]))
        queue = list(copies)
        for _ in range(6):
            queue.pop(0).start()

        def wait(count):
            for _ in range(count):
                copies.pop(0).wait()
                if queue:
                    queue.pop(0).start()

        wait(2)
        min_t[...] = v_min[...].T
        for k, t in enumerate(tiles):
            wait(3 if k == 0 else 2)
            cols = slice(k * TILE, (k + 1) * TILE)
            pre = mm(v_min[...], v_in[:, cols]) + v_bias[:, t * TILE : (t + 1) * TILE].astype(f32)
            phi = 0.5 + 0.5 * lax.erf(pre * (2.0**-0.5))
            act[:, cols] = (pre * phi).astype(bf16)
            slope = phi + pre * jnp.exp(-0.5 * pre * pre) * 0.3989422804014327
            grad_pre = slope * mm_nt(v_g[...], v_out[cols, :])
            gbias[:, cols] = jnp.sum(grad_pre, axis=0, keepdims=True)
            low[:, cols] = grad_pre.astype(bf16)
            grad_in = mm(min_t[...], low[:, cols]).astype(bf16)
            grad_out = mm_tn(act[:, cols], v_g[...]).astype(bf16)
            store_blocks(first, flip, cols, grad_in)
            spot = slice((k % 3) * 16, (k % 3 + 1) * 16)
            for w in range(8):
                slot = ((k // 3) * 8 + w) ^ flip
                second[slot, spot, 0:D] = grad_out[w * 32 : w * 32 + 16, :]
                second[slot, spot, D : 2 * D] = grad_out[w * 32 + 16 : w * 32 + 32, :]
        staging.send(plan[CORE])
        wait(len(copies))
        if carried:
            v_gn[...] += mm_nt(low[...], v_in[...])
        else:
            v_gn[...] = mm_nt(low[...], v_in[...])
        back = pltpu.make_async_copy(v_gn, o_gn, sems.at[17])
        back.start()
        if carried:
            v_acc[...] += mm(act[...], v_out[...])
        else:
            v_acc[...] = mm(act[...], v_out[...])
        more = [
            pltpu.make_async_copy(v_acc, o_acc, sems.at[18]),
            pltpu.make_async_copy(gbias, o_bias, sems.at[19]),
        ]
        for copy in more:
            copy.start()
        for copy in [back] + more:
            copy.wait()
        staging.wait()

    half = 6 * TILE
    ins = [min_, g, b_in.reshape(1, FF), w_in, w_out] + ([acc, gn] if carried else [])
    return pl.pallas_call(
        kernel,
        out_shape=[sds((rows, D), f32), sds((rows, D), f32), sds((1, half), f32)] + [sds(*o) for o in CHUNK_OUTS],
        in_specs=[SM] + [ANY] * len(ins),
        out_specs=[ANY] * (4 + CORE_PARTS),
        scratch_shapes=[
            pltpu.VMEM((rows, D), bf16),
            pltpu.VMEM((rows, D), bf16),
            pltpu.VMEM((1, FF), bf16),
            pltpu.VMEM((D, half), bf16),
            pltpu.VMEM((half, D), bf16),
            pltpu.VMEM((rows, D), f32),
            pltpu.VMEM((rows, D), f32),
            pltpu.VMEM((1, half), f32),
            pltpu.VMEM((rows, half), bf16),
            pltpu.VMEM((rows, half), bf16),
            pltpu.VMEM((D, rows), bf16),
        ]
        + chunk_extra()
        + [pltpu.SemaphoreType.DMA((20,))],
        compiler_params=params(),
        cost_estimate=cost(),
        name="mlp",
    )(plan, *ins)


def cross_scores_back(acc, gn, two, g, gain, b_out, w_cross, mix, probs, kv, cq):
    rows = cq.shape[0]
    images = rows // (2 * SEQ)

    def body(smem, load, out, send, extra):
        hid_out, gtwo, gcross, gcq, gkv, small_out = out
        low, gmix = extra
        two, gn, g, gain = load(0), load(1), load(2), load(3)
        gain2 = gain[2:3, :].astype(f32)
        sums = [jnp.zeros((1, D), f32) for _ in range(3)]
        for i in range(rows // SEQ):
            span = slice(i * SEQ, (i + 1) * SEQ)
            up = g[span, :].astype(f32)
            grad = gn[span, :]
            xhat, inv = normed(two[span, :])
            sums[0] += jnp.sum(grad * xhat, axis=0, keepdims=True)
            sums[1] += jnp.sum(grad, axis=0, keepdims=True)
            sums[2] += jnp.sum(up, axis=0, keepdims=True)
            total = up + norm_back(grad, xhat, inv, gain2)
            gtwo[span, :] = total
            low[span, :] = total.astype(bf16)
        small_out[...] = jnp.concatenate(sums + [jnp.zeros((5, D), f32)])
        send(1)
        send(5)
        gmix[...] = mm_nt(low[...], load(4)[...]).astype(bf16)
        cq, kv, probs = load(5), load(6), load(7)
        scaled = lane_masks(SCALE)
        plain = lane_masks(1.0)

        def attend(p):
            span = slice(p * 2 * SEQ, (p + 1) * 2 * SEQ)
            toks = slice(p * IMG_TOK, (p + 1) * IMG_TOK)
            for h in range(PAIRS):
                at = 2 * HEAD_DIM * h
                q = two_heads(cq[span, at : at + 128], scaled)
                gm = two_heads(gmix[span, at : at + 128], plain)
                k = kv[toks, at : at + 128]
                v = kv[toks, D + at : D + at + 128]
                pl_ = probs[p, h]
                pf = pl_.astype(f32)
                gp = mm_nt(gm, v)
                delta = jnp.sum(pf * gp, axis=-1, keepdims=True)
                gs = (pf * (gp - delta)).astype(bf16)
                gcq[span, at : at + 128] = (join_heads(mm(gs, k), 2 * SEQ) * SCALE).astype(bf16)
                gkv[toks, at : at + 128] = mm_tn(gs, q).astype(bf16)
                gkv[toks, D + at : D + at + 128] = mm_tn(pl_, gm).astype(bf16)

        unrolled(images, attend)
        send(3)
        send(4)
        gcross[...] = mm_tn(load(8)[...], low[...]).astype(bf16)
        send(2)
        bias_out = load(9)[...].astype(f32)
        acc = load(10)
        for i in range(rows // SEQ):
            span = slice(i * SEQ, (i + 1) * SEQ)
            hid_out[i] = (two[span, :] + (acc[span, :] + bias_out)).astype(bf16)

    return staged(
        "cross_scores_back",
        body,
        [],
        [two, gn, g, gain, w_cross, cq, kv, probs, mix, b_out.reshape(1, D), acc],
        [
            ((rows // SEQ, SEQ, D), bf16),
            ((rows, D), f32),
            ((D, D), bf16),
            ((rows, D), bf16),
            (kv.shape, bf16),
            ((8, D), f32),
        ],
        [pltpu.VMEM((rows, D), bf16), pltpu.VMEM((rows, D), bf16)],
    )


def cross_weights_back(plan, gcross, gcq, gkv, gtwo, one, gain, w_query, w_kv, cin, own, other):
    rows = gcq.shape[0]
    images = rows // (2 * SEQ)
    each = other.shape[0] // images
    has = IMG_TOK - each

    def body(smem, load, out, send, extra, chunk):
        (plan,) = smem
        gone_out, gimg_out, small_out = out
        tokens, sems = extra
        flip = plan[FLIP]
        copies = []
        for p in range(images):
            at = p * IMG_TOK
            copies.append(
                pltpu.make_async_copy(
                    load(8).at[pl.ds(p * each, each), :], tokens.at[pl.ds(at + has, each), :], sems.at[2 * p]
                )
            )
            if has:
                copies.append(
                    pltpu.make_async_copy(
                        load(9).at[pl.ds(p * has, has), :], tokens.at[pl.ds(at, has), :], sems.at[2 * p + 1]
                    )
                )
        for copy in copies:
            copy.start()
        gcq, cin = load(0), load(1)
        grad_query = mm_tn(cin[...], gcq[...]).astype(bf16)
        store_blocks(chunk.first, flip, slice(D, 2 * D), grad_query)
        gone_out[...] = mm_nt(gcq[...], load(2)[...])
        gkv = load(3)
        for copy in copies:
            copy.wait()
        for j in range(2):
            cols = slice(j * D, (j + 1) * D)
            store_blocks(chunk.second, flip, cols, mm_tn(tokens[...], gkv[:, cols]).astype(bf16))
        store_blocks(chunk.first, flip, slice(0, D), load(4)[...])
        chunk.send(plan[CORE])
        one, gain, gtwo = load(5), load(6), load(7)
        gain1 = gain[1:2, :].astype(f32)
        sums = [jnp.zeros((1, D), f32) for _ in range(2)]
        for i in range(rows // SEQ):
            span = slice(i * SEQ, (i + 1) * SEQ)
            grad = gone_out[span, :]
            xhat, inv = normed(one[span, :])
            sums[0] += jnp.sum(grad * xhat, axis=0, keepdims=True)
            sums[1] += jnp.sum(grad, axis=0, keepdims=True)
            gone_out[span, :] = gtwo[span, :] + norm_back(grad, xhat, inv, gain1)
        small_out[...] = jnp.concatenate(sums + [jnp.zeros((6, D), f32)])
        send(0)
        send(2)
        gimg_out[...] = mm_nt(gkv[...], load(10)[...])

    dummy = other if own is None else own
    return staged(
        "cross_weights_back",
        body,
        [plan],
        [gcq, cin, w_query, gkv, gcross, one, gain, gtwo, other, dummy, w_kv],
        [((rows, D), f32), ((images * IMG_TOK, D), f32), ((8, D), f32)],
        [pltpu.VMEM((images * IMG_TOK, D), bf16), pltpu.SemaphoreType.DMA((2 * images,))],
        late=(8, 9),
        chunk=True,
    )


def self_scores_back(gone, qkv, probs, mix, w_self):
    rows = gone.shape[0]

    def body(smem, load, out, send, extra):
        gself, gqkv = out
        low, gmix = extra
        low[...] = load(0)[...].astype(bf16)
        gmix[...] = mm_nt(low[...], load(1)[...]).astype(bf16)
        qkv, probs = load(2), load(3)
        scaled = lane_masks(SCALE)
        plain = lane_masks(1.0)

        def attend(p):
            span = slice(p * 2 * SEQ, (p + 1) * 2 * SEQ)
            for h in range(PAIRS):
                at = 2 * HEAD_DIM * h
                q = two_heads(qkv[span, at : at + 128], scaled)
                gm = two_heads(gmix[span, at : at + 128], plain)
                k = qkv[span, D + at : D + at + 128]
                v = qkv[span, 2 * D + at : 2 * D + at + 128]
                pl_ = probs[p, h]
                pf = pl_.astype(f32)
                gp = mm_nt(gm, v)
                delta = jnp.sum(pf * gp, axis=-1, keepdims=True)
                gs = (pf * (gp - delta)).astype(bf16)
                gqkv[span, at : at + 128] = (join_heads(mm(gs, k), 2 * SEQ) * SCALE).astype(bf16)
                gqkv[span, D + at : D + at + 128] = mm_tn(gs, q).astype(bf16)
                gqkv[span, 2 * D + at : 2 * D + at + 128] = mm_tn(pl_, gm).astype(bf16)

        unrolled(rows // (2 * SEQ), attend)
        send(1)
        gself[...] = mm_tn(load(4)[...], low[...]).astype(bf16)

    return staged(
        "self_scores_back",
        body,
        [],
        [gone, w_self, qkv, probs, mix],
        [((D, D), bf16), ((rows, 3 * D), bf16)],
        [pltpu.VMEM((rows, D), bf16), pltpu.VMEM((rows, D), bf16)],
    )


def self_weights_back(plan, gself, gqkv, gone, x, attn, gain, w_qkv, small1, small2, biases):
    rows = x.shape[0]
    third = 3 * TILE

    def body(smem, load, out, send, extra, chunk):
        (plan,) = smem
        hid_out, small_out = out
        (gbase,) = extra
        flip = plan[FLIP]
        attn, gqkv = load(0), load(1)
        for j in range(3):
            grad = mm_tn(attn[...], gqkv[:, j * D : (j + 1) * D]).astype(bf16)
            if j == 0:
                store_blocks(chunk.first, flip, slice(D, 2 * D), grad)
            else:
                store_blocks(chunk.second, flip, slice((j - 1) * D, j * D), grad)
        store_blocks(chunk.first, flip, slice(0, D), load(2)[...])
        chunk.send(plan[CORE])
        gbase[...] = mm_nt(gqkv[...], load(3)[...])
        x, gone, gain = load(4), load(5), load(6)
        gain0 = gain[0:1, :].astype(f32)
        sums = [jnp.zeros((1, D), f32) for _ in range(2)]
        for i in range(rows // SEQ):
            span = slice(i * SEQ, (i + 1) * SEQ)
            grad = gbase[span, :]
            xhat, inv = normed(x[span, :].astype(f32))
            sums[0] += jnp.sum(grad * xhat, axis=0, keepdims=True)
            sums[1] += jnp.sum(grad, axis=0, keepdims=True)
            hid_out[i] = gone[span, :] + norm_back(grad, xhat, inv, gain0)
        small1, small2, bias_a, bias_b = load(7), load(8), load(9), load(10)
        small_out[...] = jnp.zeros_like(small_out)
        rows_of = [sums[0], small1[0:1, :], small2[0:1, :], sums[1], small1[1:2, :], small2[1:2, :], small2[2:3, :]]
        for i, row in enumerate(rows_of + [b[:, n * third : (n + 1) * third] for n in range(2) for b in (bias_a, bias_b)]):
            small_out[i : i + 1, :] = row

    return staged(
        "self_weights_back",
        body,
        [plan],
        [attn, gqkv, gself, w_qkv, x, gone, gain, small1, small2, *biases],
        [((rows // SEQ, SEQ, D), f32), ((16, D), f32)],
        [pltpu.VMEM((rows, D), f32)],
        chunk=True,
    )


def swap(value, axis, bit):
    size = lax.axis_size(axis)
    return lax.ppermute(value, axis, [(i, i ^ bit) for i in range(size)])


def add(a, b):
    return (a.astype(f32) + b.astype(f32)).astype(bf16)


STEPS = (("narrow", 1), ("wide", 2), ("wide", 4), ("wide", 8))
X_PARTS = 1
ORDER = (
    "K0", "K1", "a", "K2", "b", "K3", "a", "K4", "a", "b", "c", "K5", "a", "b", "a", "b", "c", "d", "s", "a",
    "b", "s", "a", "c", "b", "s", "c", "s", "a", "d", "c", "s", "c", "d", "Ph", "b", "d", "c", "d", "Pi",
    "b", "Fm", "d", "c", "d", "Pg", "Fc", "d", "Fd",
)


def after(token, *values):
    tied = lax.optimization_barrier((token,) + values)[1:]
    return tied[0] if len(values) == 1 else tied


class Chunk:
    def __init__(self, keep, *send, steps=STEPS, parts=X_PARTS):
        self.keep, self.steps, self.parts = keep, steps, parts
        self.back = [s for s in steps[::-1] if s[0] == "wide"]
        self.at = 0
        self.got = [swap(part, "wide", 1) for part in send]
        self.next = 0

    def advance(self, token):
        if self.at and self.next < len(self.got) - 1:
            self.got[self.next] = after(token, self.got[self.next])
            self.next += 1
            return self.got[self.next - 1]
        keep, *got = after(token, self.keep, *self.got)
        self.next = 0
        if not self.at:
            got = [jnp.concatenate(got)]
        if self.at < len(self.steps):
            axis, bit = self.steps[self.at]
            half = keep.shape[0] // 2
            if len(got) == 1:
                parts = self.parts if self.at == 0 else 1
                size = half // parts
                spans = [slice(half + i * size, half + (i + 1) * size) for i in range(parts)]
                out = [add(keep[span], got[0][span]) for span in spans]
                self.keep = add(keep[:half], got[0][:half])
            else:
                out = [add(keep[half:], got[1])]
                self.keep = add(keep[:half], got[0])
        else:
            whole = add(keep, got[0]) if self.at == len(self.steps) else jnp.concatenate([keep, got[0]])
            spot = self.at - len(self.steps)
            axis, bit = self.back[spot] if spot < len(self.back) else ("wide", 1)
            self.keep = whole
            out = [whole]
        self.at += 1
        self.got = [swap(part, axis, bit) for part in out]
        return out[-1]

    def done(self, token):
        return after(token, self.keep, *self.got)


class Small:
    def __init__(self, value):
        self.value = value
        self.steps = (("wide", 1),) + STEPS
        self.at = 0
        self.got = swap(value, *self.steps[0])

    def advance(self, token):
        value, got = after(token, self.value, self.got)
        self.value = value + got
        self.at += 1
        if self.at < len(self.steps):
            self.got = swap(self.value, *self.steps[self.at])
        return self.value


def load_piece(plan, mine, theirs, half, index, store):
    slot = index ^ (plan[FLIP] % 8)
    core = plan[CORE]

    @pl.when(core == half)
    def _():
        store(mine[slot].astype(f32))

    @pl.when(core != half)
    def _():
        store(theirs[slot].astype(f32))


def finish_columns_kernel(cuts, plan, mine, theirs, *outs):
    for w in range(8):
        for half in range(2):

            def store(value, half=half, w=w):
                for number, src, dst, width in cuts[half]:
                    outs[number][w * BLOCK : (w + 1) * BLOCK, dst : dst + width] = value[:, src : src + width]

            load_piece(plan, mine, theirs, half, w, store)


def finish_columns(plan, pieces, cuts, widths, name):
    return pl.pallas_call(
        functools.partial(finish_columns_kernel, cuts),
        out_shape=[sds((8 * BLOCK, width), f32) for width in widths],
        in_specs=[SM, VM, VM],
        out_specs=[VM] * len(widths),
        compiler_params=params(24),
        cost_estimate=cost(0, 8e6),
        name=name,
    )(plan, *pieces)


def finish_mlp_kernel(plan, mine_a, theirs_a, mine_b, theirs_b, grad_in, grad_out):
    for call, mine, theirs in ((0, mine_a, theirs_a), (1, mine_b, theirs_b)):
        for w in range(8):

            def first(value, w=w, call=call):
                rows = slice(w * BLOCK, (w + 1) * BLOCK)
                for n in range(2):
                    dst = n * 6 * TILE + call * 3 * TILE
                    grad_in[rows, dst : dst + 3 * TILE] = value[:, n * D : (n + 1) * D]

            def second(value, w=w, call=call):
                for j in range(3):
                    for half in range(2):
                        dst = (3 * call + j) * TILE + w * 32 + half * 16
                        grad_out[dst : dst + 16, :] = value[j * 16 : (j + 1) * 16, half * D : (half + 1) * D]

            load_piece(plan, mine, theirs, 0, w, first)
            load_piece(plan, mine, theirs, 1, w, second)


def finish_mlp(plan, a, b):
    return pl.pallas_call(
        finish_mlp_kernel,
        out_shape=[sds((8 * BLOCK, FF), f32), sds((FF // 2, D), f32)],
        in_specs=[SM] + [VM] * 4,
        out_specs=[VM] * 2,
        compiler_params=params(40),
        cost_estimate=cost(0, 16e6),
        name="finish_mlp",
    )(plan, *a, *b)


def plain_sum(value):
    shard = lax.psum_scatter(value, "narrow", scatter_dimension=0, tiled=True)
    return lax.psum(shard, "wide").astype(f32)


def plain_sums(core, chunks):
    whole = []
    for keep, *send in chunks:
        send = jnp.concatenate(send)
        first = jnp.where(core == 0, keep, send)
        second = jnp.where(core == 0, send, keep)
        whole.append((first.reshape(D, WIDE_COLS), second))
    grad_in = jnp.stack([whole[0][0].reshape(D, 2, 3 * TILE), whole[1][0].reshape(D, 2, 3 * TILE)], axis=2)
    grad_out = jnp.stack([whole[0][1], whole[1][1]]).reshape(2, 2, 8, 3, 16, 2, D)
    grad_out = grad_out.transpose(1, 0, 3, 2, 5, 4, 6).reshape(FF, D)
    crosses, keys = whole[2][0], whole[2][1].reshape(D, WIDE_COLS)
    front_half, back_half = whole[3][0], whole[3][1].reshape(D, WIDE_COLS)
    return [
        plain_sum(v)
        for v in (
            jnp.concatenate([front_half[:, D:], back_half], axis=1),
            front_half[:, :D],
            crosses[:, D:],
            keys,
            crosses[:, :D],
            grad_in.reshape(D, FF),
            grad_out,
        )
    ]


def local(
    hidden_in, image_tokens, image_group, caption_len, norm_gain, norm_bias, self_qkv, self_out, cross_query,
    cross_kv, cross_out, mlp_in, mlp_bias_in, mlp_out, mlp_bias_out, out_grad,
):
    narrow = lax.axis_size("narrow")
    wide = lax.axis_size("wide")
    images, toks, _ = image_tokens.shape
    mine = images // narrow
    caps = 2 * mine
    rows = caps * SEQ
    n_at, w_at = lax.axis_index("narrow"), lax.axis_index("wide")
    fast = narrow == 2 and wide == 16
    core = w_at % 2
    if fast:
        flip = n_at * 8 + (w_at // 2) % 2 * 4 + (w_at // 4) % 2 * 2 + (w_at // 8) % 2
    else:
        flip = jnp.zeros_like(n_at)
    pos = jnp.stack([n_at, w_at * images, flip, core]).astype(jnp.int32)
    plan = make_plan(narrow, images, image_group, caption_len, pos)
    if narrow == 2:
        own, away = pick_tokens(plan, image_tokens, mine)
        got = swap(away, "narrow", 1)
        own = own.reshape(mine * toks, D)
        other = got.reshape(mine * toks, D)
    else:
        every = lax.all_gather(image_tokens, "narrow")
        first = n_at * mine
        tokens = lax.dynamic_slice_in_dim(every, first, mine, 1).transpose(1, 0, 2, 3)
        own, other = None, tokens.reshape(mine * IMG_TOK, D)
    x, attn, qkv, self_probs, self_mix, one, cin, cq, kv_own = front(
        rows, plan, hidden_in, out_grad, norm_gain, norm_bias, self_qkv, self_out, cross_query, own, cross_kv
    )
    kv, cross_probs, cross_mix, two, min_, g = cross(
        plan, kv_own, other, cq, one, norm_gain, norm_bias, cross_kv, cross_out, out_grad
    )
    state = {}
    token = min_

    def first_half(tie):
        acc, gn, bias, *chunk = mlp(0, plan, min_, g, None, None, mlp_in, mlp_bias_in, mlp_out)
        state.update(acc=acc, gn=gn, bias0=bias, a=chunk)
        return bias

    def second_half(tie):
        acc, gn = tie(state["acc"], state["gn"])
        acc, gn, bias, *chunk = mlp(1, plan, min_, g, acc, gn, mlp_in, mlp_bias_in, mlp_out)
        state.update(acc=acc, gn=gn, bias1=bias, b=chunk)
        return bias

    def cross_one(tie):
        acc, gn = tie(state["acc"], state["gn"])
        hidden_out, gtwo, gcross, gcq, gkv, small = cross_scores_back(
            acc, gn, two, g, norm_gain, mlp_bias_out, cross_out, cross_mix, cross_probs, kv, cq
        )
        state.update(hidden_out=hidden_out, gtwo=gtwo, gcross=gcross, gcq=gcq, gkv=gkv, small2=small)
        return small

    def cross_two(tie):
        gcq, gkv = tie(state["gcq"], state["gkv"])
        gone, gimg, small, *chunk = cross_weights_back(
            plan, state["gcross"], gcq, gkv, state["gtwo"], one, norm_gain, cross_query, cross_kv, cin, own, other
        )
        state.update(gone=gone, gimg=gimg, small1=small, c=chunk)
        return small

    def self_one(tie):
        gone, low_ = tie(state["gone"], self_mix)
        gself, gqkv = self_scores_back(gone, qkv, self_probs, low_, self_out)
        state.update(gself=gself, gqkv=gqkv)
        return gself

    def self_two(tie):
        gself, gqkv = tie(state["gself"], state["gqkv"])
        grad_hidden, small, *chunk = self_weights_back(
            plan, gself, gqkv, state["gone"], x, attn, norm_gain, self_qkv, state["small1"], state["small2"],
            (state["bias0"], state["bias1"]),
        )
        state.update(grad_hidden=grad_hidden, d=chunk, s=small)
        return small

    def place_out(token):
        away = swap(state["hidden_out"].reshape(mine, 2, SEQ, D)[:, 1], "narrow", 1)
        return place(OUT_SRC, caps, plan, state["hidden_out"], after(token, away), bf16, "place_out")

    def place_grad(token):
        away = swap(state["grad_hidden"].reshape(mine, 2, SEQ, D)[:, 1].astype(bf16), "narrow", 1)
        return place(OUT_SRC, caps, plan, state["grad_hidden"], after(token, away), f32, "place_grad")

    def place_image(token):
        whole = state["gimg"].reshape(mine, IMG_TOK, D)
        away = swap(whole[:, toks:].astype(bf16), "narrow", 1)
        return place(IMG_SRC, images, plan, whole[:, :toks], after(token, away), f32, "place_image")

    def finish_two(token):
        return finish_mlp(plan, live["a"].done(token), live["b"].done(token))

    def finish_cross(token):
        cuts = (((0, 0, 0, D), (1, D, 0, D)), ((2, 0, 0, 2 * D),))
        return finish_columns(plan, live["c"].done(token), cuts, (D, D, 2 * D), "finish_cross")

    def finish_self(token):
        cuts = (((0, 0, 0, D), (1, D, 0, D)), ((1, 0, D, 2 * D),))
        return finish_columns(plan, live["d"].done(token), cuts, (D, 3 * D), "finish_self")

    live = {}
    last = {"Ph": place_out, "Pg": place_grad, "Pi": place_image, "Fm": finish_two, "Fc": finish_cross, "Fd": finish_self}
    kernels = {
        "K0": first_half, "K1": second_half, "K2": cross_one, "K3": cross_two, "K4": self_one, "K5": self_two
    }
    if fast:
        for event in ORDER:
            if event in kernels:
                token = kernels[event](functools.partial(after, token))
                for name in "abcd":
                    if name in state:
                        live[name] = Chunk(*state.pop(name))
                if "s" in state:
                    live["s"] = Small(state.pop("s"))
            elif event in last:
                state[event] = last[event](token)
                token = jax.tree.leaves(state[event])[0]
            else:
                token = live[event].advance(token)
        final_out, final_grad, grad_image = state["Ph"], state["Pg"], state["Pi"]
        grad_mlp_in, grad_mlp_out = state["Fm"]
        grad_cross_out, grad_query, grad_kv = state["Fc"]
        grad_self_out, grad_qkv = state["Fd"]
        small = live["s"].value
    else:
        for kernel in kernels.values():
            kernel(lambda *values: values)
        grad_qkv, grad_self_out, grad_query, grad_kv, grad_cross_out, grad_mlp_in, grad_mlp_out = plain_sums(
            core, [state[name] for name in "abcd"]
        )
        small = lax.psum(state["s"], ("wide", "narrow"))
        out_all = lax.all_gather(state["hidden_out"], "narrow", tiled=True)
        grad_all = lax.all_gather(state["grad_hidden"].astype(bf16), "narrow", tiled=True)
        final_out = place(OUT_SRC, caps, plan, out_all, out_all[:1], bf16, "place_out")
        final_grad = place(OUT_SRC, caps, plan, grad_all, grad_all[:1], f32, "place_grad")
        every = lax.all_gather(state["gimg"].reshape(mine, IMG_TOK, D).astype(bf16), "narrow", tiled=True)
        grad_image = lax.dynamic_slice_in_dim(every, n_at * toks, toks, 1).astype(f32)
    share = D // narrow
    columns = lax.dynamic_slice_in_dim(small[:7], n_at * share, share, 1)
    grad_bias_in = lax.dynamic_slice_in_dim(small[7:11].reshape(FF), n_at * (FF // narrow), FF // narrow, 0)
    return (
        final_out.reshape(rows, D),
        final_grad.reshape(rows, D),
        grad_image,
        columns[:3],
        columns[3:6],
        grad_qkv,
        grad_self_out,
        grad_query,
        grad_kv,
        grad_cross_out,
        grad_mlp_in,
        grad_bias_in,
        grad_mlp_out,
        columns[6],
    )


def solution(mesh):
    in_specs = (
        P("wide", None),
        P("wide", "narrow", None),
        P("wide"),
        P("wide"),
    ) + (P(),) * 11 + (P("wide", None),)
    out_specs = (
        P(("wide", "narrow"), None),
        P(("wide", "narrow"), None),
        P("wide", "narrow", None),
        P(None, "narrow"),
        P(None, "narrow"),
        P("narrow", None),
        P("narrow", None),
        P("narrow", None),
        P("narrow", None),
        P("narrow", None),
        P("narrow", None),
        P("narrow"),
        P("narrow", None),
        P("narrow"),
    )
    return jax.shard_map(local, mesh=mesh, in_specs=in_specs, out_specs=out_specs, check_vma=False)
```

```python
import functools

import jax
import jax.numpy as jnp
from jax import lax
from jax.experimental import pallas as pl
from jax.experimental.pallas import tpu as pltpu
from jax.sharding import PartitionSpec as P

D = 768
HEADS = 12
HEAD_DIM = 64
FF = 3072
SEQ = 64
IMG_TOK = 256
PAIRS = HEADS // 2
SCALE = HEAD_DIM**-0.5
BLOCK = 48
BLOCKS = D // BLOCK
WIDE_COLS = 2 * D
TILE = 256
f32 = jnp.float32
bf16 = jnp.bfloat16
VM = pl.BlockSpec(memory_space=pltpu.VMEM)
SM = pl.BlockSpec(memory_space=pltpu.SMEM)
ANY = pl.BlockSpec(memory_space=pl.ANY)
CORE_PARTS = 4
CAPS, LENS, MINE, PEER, IMG_SRC, OUT_SRC, FLIP, CORE, PLAN = 0, 8, 16, 20, 24, 32, 40, 41, 48


def mm(left, right):
    return lax.dot_general(left, right, (((1,), (0,)), ((), ())), preferred_element_type=f32)


def mm_nt(left, right):
    return lax.dot_general(left, right, (((1,), (1,)), ((), ())), preferred_element_type=f32)


def mm_tn(left, right):
    return lax.dot_general(left, right, (((0,), (0,)), ((), ())), preferred_element_type=f32)


def params(vmem=56, grid=None):
    return pltpu.CompilerParams(
        vmem_limit_bytes=vmem * 1024 * 1024,
        dimension_semantics=None if grid is None else ("arbitrary",) * grid,
    )


def cost(*_):
    return pl.CostEstimate(flops=1024, bytes_accessed=1024, transcendentals=0)


def sds(shape, dtype):
    return jax.ShapeDtypeStruct(shape, dtype)


def normed(x):
    center = x - jnp.mean(x, axis=-1, keepdims=True)
    inv = lax.rsqrt(jnp.mean(center * center, axis=-1, keepdims=True) + 1e-05)
    return center * inv, inv


def norm_back(grad, xhat, inv, gain):
    u = grad * gain
    return inv * (
        u - jnp.mean(u, axis=-1, keepdims=True) - xhat * jnp.mean(u * xhat, axis=-1, keepdims=True)
    )


def lane_masks(scale):
    lane = lax.broadcasted_iota(jnp.int32, (1, 2 * HEAD_DIM), 1)
    low = jnp.where(lane < HEAD_DIM, scale, 0.0).astype(bf16)
    high = jnp.where(lane < HEAD_DIM, 0.0, scale).astype(bf16)
    return low, high


def two_heads(x, masks):
    return jnp.concatenate([x * masks[0], x * masks[1]], axis=0)


def join_heads(x, rows):
    lane = lax.broadcasted_iota(jnp.int32, (rows, 2 * HEAD_DIM), 1)
    return jnp.where(lane < HEAD_DIM, x[:rows], x[rows:])


def plan_kernel(narrow, images, group, lens, pos, out, place, count):
    me = pos[0]
    base = pos[1]
    half = images // narrow
    caps = 2 * images
    for p in range(images):
        count[p] = 0
    for c in range(caps):
        g = group[c] - base
        n = count[g]
        place[2 * g + n] = c
        count[g] = n + 1
    for i in range(PLAN):
        out[i] = 0
    out[FLIP] = pos[2]
    out[CORE] = pos[3]
    slots = [jnp.int32(0) for _ in range(2)]
    turn = jnp.int32(0)
    for p in range(images):
        a = place[2 * p]
        b = place[2 * p + 1]
        if narrow == 2:
            both_low = b < images
            both_high = a >= images
            mixed = jnp.logical_not(jnp.logical_or(both_low, both_high))
            owner = jnp.where(both_low, 0, jnp.where(both_high, 1, turn))
            turn = jnp.where(mixed, 1 - turn, turn)
            slot = jnp.where(owner == 0, slots[0], slots[1])
            slots[0] = jnp.where(owner == 0, slots[0] + 1, slots[0])
            slots[1] = jnp.where(owner == 1, slots[1] + 1, slots[1])
            swap = jnp.logical_and(mixed, owner == 1)
            first = jnp.where(swap, b, a)
            second = jnp.where(swap, a, b)
            mine = owner == me

            @pl.when(mine)
            def _():
                out[MINE + slot] = p
                out[CAPS + 2 * slot] = first
                out[CAPS + 2 * slot + 1] = second
                out[LENS + 2 * slot] = lens[first]
                out[LENS + 2 * slot + 1] = lens[second]

            @pl.when(jnp.logical_not(mine))
            def _():
                out[PEER + slot] = p

            out[IMG_SRC + p] = jnp.where(mine, slot, half + slot)
            for k, c in ((0, first), (1, second)):

                @pl.when(c // images == me)
                def _():
                    out[OUT_SRC + c - me * images] = jnp.where(mine, 2 * slot + k, caps // 2 + slot)

        else:
            owner = p // half
            slot = p % half
            mine = owner == me
            per = caps // narrow

            @pl.when(mine)
            def _():
                out[MINE + slot] = p
                for k, c in ((0, a), (1, b)):
                    out[CAPS + 2 * slot + k] = c
                    out[LENS + 2 * slot + k] = lens[c]

            for k, c in ((0, a), (1, b)):

                @pl.when(c // per == me)
                def _():
                    out[OUT_SRC + c - me * per] = 2 * p + k


def make_plan(narrow, images, group, lens, pos):
    return pl.pallas_call(
        functools.partial(plan_kernel, narrow, images),
        out_shape=sds((PLAN,), jnp.int32),
        in_specs=[SM, SM, SM],
        out_specs=SM,
        scratch_shapes=[
            pltpu.SMEM((2 * images,), jnp.int32),
            pltpu.SMEM((images,), jnp.int32),
        ],
        compiler_params=params(4),
        name="plan",
    )(group, lens, pos)


def pick_kernel(plan, tokens_a, tokens_b, mine, peer):
    mine[...] = tokens_a[...]
    peer[...] = tokens_b[...]


def pick_tokens(plan, tokens, count):
    block = (1,) + tokens.shape[1:]
    return pl.pallas_call(
        pick_kernel,
        grid_spec=pltpu.PrefetchScalarGridSpec(
            num_scalar_prefetch=1,
            grid=(count,),
            in_specs=[
                pl.BlockSpec(block, lambda i, plan: (plan[MINE + i], 0, 0)),
                pl.BlockSpec(block, lambda i, plan: (plan[PEER + i], 0, 0)),
            ],
            out_specs=[pl.BlockSpec(block, lambda i, plan: (i, 0, 0))] * 2,
        ),
        out_shape=[sds((count,) + tokens.shape[1:], bf16)] * 2,
        compiler_params=params(8),
        name="pick",
    )(plan, tokens, tokens)


def place_kernel(offset, count, plan, own, got, out):
    have = own.shape[0]
    for i in range(count):
        src = plan[offset + i]

        @pl.when(src < have)
        def _():
            out[i] = own[jnp.minimum(src, have - 1)].astype(out.dtype)

        @pl.when(src >= have)
        def _():
            out[i] = got[jnp.maximum(src - have, 0)].astype(out.dtype)


def place(offset, count, plan, own, got, dtype, name):
    return pl.pallas_call(
        functools.partial(place_kernel, offset, count),
        out_shape=sds((count,) + own.shape[1:], dtype),
        in_specs=[SM, VM, VM],
        out_specs=VM,
        compiler_params=params(24),
        cost_estimate=cost(0, 4 * count * own.shape[1] * own.shape[2] * 2),
        name=name,
    )(plan, own, got)


WINDOW = 4


def staged(name, body, smem, ins, outs, extra=(), late=(), chunk=False, vmem=56):
    n_s, n_i, n_o, n_e = len(smem), len(ins), len(outs), len(extra)
    n_c = 1 + CORE_PARTS if chunk else 0
    staged_ins = [i for i in range(n_i) if i not in late]

    def kernel(*refs):
        refs = list(refs)
        take = lambda n: [refs.pop(0) for _ in range(n)]
        scalars, h_in, h_out = take(n_s), take(n_i), take(n_o)
        chunk_out = take(n_c)
        v_in = dict(zip(staged_ins, take(len(staged_ins))))
        v_out, more = take(n_o), take(n_e)
        staging = Staging(chunk_out, *take(3)) if chunk else None
        in_sem, out_sem = refs
        copies = {i: pltpu.make_async_copy(h_in[i], v_in[i], in_sem.at[i]) for i in staged_ins}
        started, waited, going = [], set(), []

        def ahead(count):
            for i in staged_ins:
                if count <= 0:
                    return
                if i not in started:
                    copies[i].start()
                    started.append(i)
                    count -= 1

        ahead(WINDOW)

        def load(i):
            if i in late:
                return h_in[i]
            if i not in waited:
                assert i in started
                copies[i].wait()
                waited.add(i)
                ahead(1)
            return v_in[i]

        def send(i):
            copy = pltpu.make_async_copy(v_out[i], h_out[i], out_sem.at[i])
            copy.start()
            going.append((i, copy))

        body(scalars, load, v_out, send, more, *([staging] if chunk else []))
        sent = {i for i, _ in going}
        for i in range(n_o):
            if i not in sent and outs[i] is not None:
                send(i)
        for i in staged_ins:
            load(i)
        for _, copy in going:
            copy.wait()
        if chunk:
            staging.wait()

    return pl.pallas_call(
        kernel,
        out_shape=[sds(*o) for o in outs] + [sds(*o) for o in CHUNK_OUTS[:n_c]],
        in_specs=[SM] * n_s + [ANY] * n_i,
        out_specs=[ANY] * (n_o + n_c),
        scratch_shapes=[pltpu.VMEM(ins[i].shape, ins[i].dtype) for i in staged_ins]
        + [pltpu.VMEM(*o) for o in outs]
        + list(extra)
        + (chunk_extra() if chunk else [])
        + [pltpu.SemaphoreType.DMA((max(n_i, 1),)), pltpu.SemaphoreType.DMA((max(n_o, 1),))],
        compiler_params=params(vmem),
        cost_estimate=cost(),
        name=name,
    )(*smem, *ins)


def unrolled(count, step):
    for i in range(count):
        step(i)


def front(rows, plan, hidden, out_grad, gain, bias, w_qkv, w_self, w_query, own, w_kv):
    pairs = rows // (2 * SEQ)
    kv_rows = 0 if own is None else own.shape[0]

    def body(smem, load, out, send, extra):
        (plan,) = smem
        x_out, attn_out, qkv_out, probs_out, mix_out, one_out, cin_out, cq_out, kv_out = out
        hidden = load(0)
        gain, bias = load(1), load(2)
        gain0, bias0 = gain[0:1, :].astype(f32), bias[0:1, :].astype(f32)
        gain1, bias1 = gain[1:2, :].astype(f32), bias[1:2, :].astype(f32)

        def gather(i):
            src = pl.ds(pl.multiple_of(plan[CAPS + i] * SEQ, SEQ), SEQ)
            dst = slice(i * SEQ, (i + 1) * SEQ)
            x = hidden[src, :]
            x_out[dst, :] = x
            attn_out[dst, :] = (normed(x.astype(f32))[0] * gain0 + bias0).astype(bf16)

        unrolled(rows // SEQ, gather)
        send(0)
        send(1)
        w_qkv = load(3)
        for j in range(3):
            cols = slice(j * D, (j + 1) * D)
            qkv_out[:, cols] = mm(attn_out[...], w_qkv[:, cols]).astype(bf16)
        send(2)
        masks = lane_masks(SCALE)
        row = lax.broadcasted_iota(jnp.int32, (2 * SEQ, 2 * SEQ), 0)
        col = lax.broadcasted_iota(jnp.int32, (2 * SEQ, 2 * SEQ), 1)
        causal = jnp.logical_and(col <= row, (col // SEQ) == (row // SEQ))

        def attend(p):
            span = slice(p * 2 * SEQ, (p + 1) * 2 * SEQ)
            length = jnp.where(col < SEQ, plan[LENS + 2 * p], plan[LENS + 2 * p + 1])
            allowed = jnp.logical_and(causal, (col % SEQ) < length)
            fill = jnp.where(allowed, 0.0, -1e30)
            fill = jnp.concatenate([fill, fill], axis=0)
            for h in range(PAIRS):
                at = 2 * HEAD_DIM * h
                q = two_heads(qkv_out[span, at : at + 128], masks)
                k = qkv_out[span, D + at : D + at + 128]
                v = qkv_out[span, 2 * D + at : 2 * D + at + 128]
                logits = jnp.where(fill < 0.0, fill, mm_nt(q, k))
                e = jnp.exp(logits - jnp.max(logits, axis=-1, keepdims=True))
                low = (e * (1.0 / jnp.sum(e, axis=-1, keepdims=True))).astype(bf16)
                probs_out[p, h] = low
                mix_out[span, at : at + 128] = join_heads(mm(low, v), 2 * SEQ).astype(bf16)

        unrolled(pairs, attend)
        send(3)
        send(4)
        one_out[...] = mm(mix_out[...], load(4)[...])

        def second(i):
            span = slice(i * SEQ, (i + 1) * SEQ)
            one = one_out[span, :] + x_out[span, :].astype(f32)
            one_out[span, :] = one
            cin_out[span, :] = (normed(one)[0] * gain1 + bias1).astype(bf16)

        unrolled(rows // SEQ, second)
        send(5)
        send(6)
        cq_out[...] = mm(cin_out[...], load(5)[...]).astype(bf16)
        send(7)
        if own is not None:
            for j in range(2):
                cols = slice(j * D, (j + 1) * D)
                kv_out[:, cols] = mm(load(6)[...], load(7)[:, cols]).astype(bf16)

    ins = [hidden, gain, bias, w_qkv, w_self, w_query] + ([] if own is None else [own, w_kv])
    return staged(
        "front",
        body,
        [plan],
        ins,
        [
            ((rows, D), bf16),
            ((rows, D), bf16),
            ((rows, 3 * D), bf16),
            ((pairs, PAIRS, 4 * SEQ, 2 * SEQ), bf16),
            ((rows, D), bf16),
            ((rows, D), f32),
            ((rows, D), bf16),
            ((rows, D), bf16),
            ((max(kv_rows, 16), 2 * D), bf16),
        ],
    )


def cross(plan, kv_own, tokens, cq, one, gain, bias, w_kv, w_cross, out_grad):
    rows = cq.shape[0]
    images = rows // (2 * SEQ)
    each = tokens.shape[0] // images
    has = IMG_TOK - each

    def body(smem, load, out, send, extra):
        (plan,) = smem
        kv_out, probs_out, mix_out, two_out, min_out, g_out = out
        raw, grads_in = extra
        gather = [
            pltpu.make_async_copy(
                load(8).at[pl.ds(pl.multiple_of(plan[CAPS + i] * SEQ, SEQ), SEQ), :],
                g_out.at[pl.ds(i * SEQ, SEQ), :],
                grads_in.at[i],
            )
            for i in range(rows // SEQ)
        ]
        for copy in gather:
            copy.start()
        tokens, w_kv = load(0), load(1)
        for j in range(2):
            cols = slice(j * D, (j + 1) * D)
            raw[:, cols] = mm(tokens[...], w_kv[:, cols]).astype(bf16)
        for p in range(images):
            kv_out[p * IMG_TOK + has : (p + 1) * IMG_TOK, :] = raw[p * each : (p + 1) * each, :]
            if has:
                kv_out[p * IMG_TOK : p * IMG_TOK + has, :] = load(2)[p * has : (p + 1) * has, :]
        send(0)
        cq = load(3)
        masks = lane_masks(SCALE)

        def attend(p):
            span = slice(p * 2 * SEQ, (p + 1) * 2 * SEQ)
            toks = slice(p * IMG_TOK, (p + 1) * IMG_TOK)
            for h in range(PAIRS):
                at = 2 * HEAD_DIM * h
                q = two_heads(cq[span, at : at + 128], masks)
                logits = mm_nt(q, kv_out[toks, at : at + 128])
                e = jnp.exp(logits - jnp.max(logits, axis=-1, keepdims=True))
                low = (e * (1.0 / jnp.sum(e, axis=-1, keepdims=True))).astype(bf16)
                probs_out[p, h] = low
                mix = mm(low, kv_out[toks, D + at : D + at + 128])
                mix_out[span, at : at + 128] = join_heads(mix, 2 * SEQ).astype(bf16)

        unrolled(images, attend)
        send(1)
        send(2)
        two_out[...] = mm(mix_out[...], load(4)[...])
        one, gain, bias = load(5), load(6), load(7)
        gain2, bias2 = gain[2:3, :].astype(f32), bias[2:3, :].astype(f32)

        def second(i):
            span = slice(i * SEQ, (i + 1) * SEQ)
            two = two_out[span, :] + one[span, :]
            two_out[span, :] = two
            min_out[span, :] = (normed(two)[0] * gain2 + bias2).astype(bf16)

        unrolled(rows // SEQ, second)
        for copy in gather:
            copy.wait()

    return staged(
        "cross",
        body,
        [plan],
        [tokens, w_kv, kv_own, cq, w_cross, one, gain, bias, out_grad],
        [
            ((images * IMG_TOK, 2 * D), bf16),
            ((images, PAIRS, 4 * SEQ, IMG_TOK), bf16),
            ((rows, D), bf16),
            ((rows, D), f32),
            ((rows, D), bf16),
            ((rows, D), bf16),
        ],
        [pltpu.VMEM((tokens.shape[0], 2 * D), bf16), pltpu.SemaphoreType.DMA((rows // SEQ,))],
        late=(8,),
    )


CHUNK_OUTS = [((BLOCKS, BLOCK, WIDE_COLS), bf16)] + [((BLOCKS // CORE_PARTS, BLOCK, WIDE_COLS), bf16)] * CORE_PARTS


def chunk_extra():
    return [
        pltpu.VMEM((BLOCKS, BLOCK, WIDE_COLS), bf16),
        pltpu.VMEM((BLOCKS, BLOCK, WIDE_COLS), bf16),
        pltpu.SemaphoreType.DMA((1 + CORE_PARTS,)),
    ]


class Staging:
    def __init__(self, outs, first, second, sems):
        self.keep, *self.parts = outs
        self.first, self.second, self.sems = first, second, sems

    def copies(self, kept, sent):
        size = BLOCKS // CORE_PARTS
        return [pltpu.make_async_copy(kept, self.keep, self.sems.at[CORE_PARTS])] + [
            pltpu.make_async_copy(sent.at[pl.ds(i * size, size)], self.parts[i], self.sems.at[i])
            for i in range(CORE_PARTS)
        ]

    def send(self, core):
        @pl.when(core == 0)
        def _():
            for copy in self.copies(self.first, self.second):
                copy.start()

        @pl.when(core != 0)
        def _():
            for copy in self.copies(self.second, self.first):
                copy.start()

    def wait(self):
        for copy in self.copies(self.first, self.second):
            copy.wait()


def store_blocks(ref, flip, cols, value):
    for b in range(BLOCKS):
        ref[b ^ flip, :, cols] = value[b * BLOCK : (b + 1) * BLOCK, :]


def mlp(call, plan, min_, g, acc, gn, w_in, b_in, w_out):
    rows = g.shape[0]
    tiles = [k + 3 * (k // 3) + 3 * call for k in range(6)]
    carried = acc is not None

    def kernel(*refs):
        refs = list(refs)
        take = lambda n: [refs.pop(0) for _ in range(n)]
        (plan,) = take(1)
        h_min, h_g, h_bias, h_in, h_out = take(5)
        h_acc, h_gn = take(2) if carried else (None, None)
        o_acc, o_gn, o_bias, o_keep = take(4)
        o_parts = take(CORE_PARTS)
        v_min, v_g, v_bias, v_in, v_out, v_acc, v_gn, gbias, act, low, min_t, first, second, chunk_sem, sems = refs
        flip = plan[FLIP]
        staging = Staging([o_keep] + o_parts, first, second, chunk_sem)
        copies = [
            pltpu.make_async_copy(h_min, v_min, sems.at[0]),
            pltpu.make_async_copy(h_bias, v_bias, sems.at[1]),
        ]
        for k, t in enumerate(tiles):
            mine, there = pl.ds(k * TILE, TILE), pl.ds(t * TILE, TILE)
            copies.append(pltpu.make_async_copy(h_in.at[:, there], v_in.at[:, mine], sems.at[2 + 2 * k]))
            copies.append(pltpu.make_async_copy(h_out.at[there, :], v_out.at[mine, :], sems.at[3 + 2 * k]))
        copies.insert(3, pltpu.make_async_copy(h_g, v_g, sems.at[14]))
        if carried:
            copies.append(pltpu.make_async_copy(h_acc, v_acc, sems.at[15]))
            copies.append(pltpu.make_async_copy(h_gn, v_gn, sems.at[16]))
        queue = list(copies)
        for _ in range(6):
            queue.pop(0).start()

        def wait(count):
            for _ in range(count):
                copies.pop(0).wait()
                if queue:
                    queue.pop(0).start()

        wait(2)
        min_t[...] = v_min[...].T
        for k, t in enumerate(tiles):
            wait(3 if k == 0 else 2)
            cols = slice(k * TILE, (k + 1) * TILE)
            pre = mm(v_min[...], v_in[:, cols]) + v_bias[:, t * TILE : (t + 1) * TILE].astype(f32)
            phi = 0.5 + 0.5 * lax.erf(pre * (2.0**-0.5))
            act[:, cols] = (pre * phi).astype(bf16)
            slope = phi + pre * jnp.exp(-0.5 * pre * pre) * 0.3989422804014327
            grad_pre = slope * mm_nt(v_g[...], v_out[cols, :])
            gbias[:, cols] = jnp.sum(grad_pre, axis=0, keepdims=True)
            low[:, cols] = grad_pre.astype(bf16)
            grad_in = mm(min_t[...], low[:, cols]).astype(bf16)
            grad_out = mm_tn(act[:, cols], v_g[...]).astype(bf16)
            store_blocks(first, flip, cols, grad_in)
            spot = slice((k % 3) * 16, (k % 3 + 1) * 16)
            for w in range(8):
                slot = ((k // 3) * 8 + w) ^ flip
                second[slot, spot, 0:D] = grad_out[w * 32 : w * 32 + 16, :]
                second[slot, spot, D : 2 * D] = grad_out[w * 32 + 16 : w * 32 + 32, :]
        staging.send(plan[CORE])
        wait(len(copies))
        if carried:
            v_gn[...] += mm_nt(low[...], v_in[...])
        else:
            v_gn[...] = mm_nt(low[...], v_in[...])
        back = pltpu.make_async_copy(v_gn, o_gn, sems.at[17])
        back.start()
        if carried:
            v_acc[...] += mm(act[...], v_out[...])
        else:
            v_acc[...] = mm(act[...], v_out[...])
        more = [
            pltpu.make_async_copy(v_acc, o_acc, sems.at[18]),
            pltpu.make_async_copy(gbias, o_bias, sems.at[19]),
        ]
        for copy in more:
            copy.start()
        for copy in [back] + more:
            copy.wait()
        staging.wait()

    half = 6 * TILE
    ins = [min_, g, b_in.reshape(1, FF), w_in, w_out] + ([acc, gn] if carried else [])
    return pl.pallas_call(
        kernel,
        out_shape=[sds((rows, D), f32), sds((rows, D), f32), sds((1, half), f32)] + [sds(*o) for o in CHUNK_OUTS],
        in_specs=[SM] + [ANY] * len(ins),
        out_specs=[ANY] * (4 + CORE_PARTS),
        scratch_shapes=[
            pltpu.VMEM((rows, D), bf16),
            pltpu.VMEM((rows, D), bf16),
            pltpu.VMEM((1, FF), bf16),
            pltpu.VMEM((D, half), bf16),
            pltpu.VMEM((half, D), bf16),
            pltpu.VMEM((rows, D), f32),
            pltpu.VMEM((rows, D), f32),
            pltpu.VMEM((1, half), f32),
            pltpu.VMEM((rows, half), bf16),
            pltpu.VMEM((rows, half), bf16),
            pltpu.VMEM((D, rows), bf16),
        ]
        + chunk_extra()
        + [pltpu.SemaphoreType.DMA((20,))],
        compiler_params=params(),
        cost_estimate=cost(),
        name="mlp",
    )(plan, *ins)


def cross_scores_back(acc, gn, two, g, gain, b_out, w_cross, mix, probs, kv, cq):
    rows = cq.shape[0]
    images = rows // (2 * SEQ)

    def body(smem, load, out, send, extra):
        hid_out, gtwo, gcross, gcq, gkv, small_out = out
        low, gmix = extra
        two, gn, g, gain = load(0), load(1), load(2), load(3)
        gain2 = gain[2:3, :].astype(f32)
        sums = [jnp.zeros((1, D), f32) for _ in range(3)]
        for i in range(rows // SEQ):
            span = slice(i * SEQ, (i + 1) * SEQ)
            up = g[span, :].astype(f32)
            grad = gn[span, :]
            xhat, inv = normed(two[span, :])
            sums[0] += jnp.sum(grad * xhat, axis=0, keepdims=True)
            sums[1] += jnp.sum(grad, axis=0, keepdims=True)
            sums[2] += jnp.sum(up, axis=0, keepdims=True)
            total = up + norm_back(grad, xhat, inv, gain2)
            gtwo[span, :] = total
            low[span, :] = total.astype(bf16)
        small_out[...] = jnp.concatenate(sums + [jnp.zeros((5, D), f32)])
        send(1)
        send(5)
        gmix[...] = mm_nt(low[...], load(4)[...]).astype(bf16)
        cq, kv, probs = load(5), load(6), load(7)
        scaled = lane_masks(SCALE)
        plain = lane_masks(1.0)

        def attend(p):
            span = slice(p * 2 * SEQ, (p + 1) * 2 * SEQ)
            toks = slice(p * IMG_TOK, (p + 1) * IMG_TOK)
            for h in range(PAIRS):
                at = 2 * HEAD_DIM * h
                q = two_heads(cq[span, at : at + 128], scaled)
                gm = two_heads(gmix[span, at : at + 128], plain)
                k = kv[toks, at : at + 128]
                v = kv[toks, D + at : D + at + 128]
                pl_ = probs[p, h]
                pf = pl_.astype(f32)
                gp = mm_nt(gm, v)
                delta = jnp.sum(pf * gp, axis=-1, keepdims=True)
                gs = (pf * (gp - delta)).astype(bf16)
                gcq[span, at : at + 128] = (join_heads(mm(gs, k), 2 * SEQ) * SCALE).astype(bf16)
                gkv[toks, at : at + 128] = mm_tn(gs, q).astype(bf16)
                gkv[toks, D + at : D + at + 128] = mm_tn(pl_, gm).astype(bf16)

        unrolled(images, attend)
        send(3)
        send(4)
        gcross[...] = mm_tn(load(8)[...], low[...]).astype(bf16)
        send(2)
        bias_out = load(9)[...].astype(f32)
        acc = load(10)
        for i in range(rows // SEQ):
            span = slice(i * SEQ, (i + 1) * SEQ)
            hid_out[i] = (two[span, :] + (acc[span, :] + bias_out)).astype(bf16)

    return staged(
        "cross_scores_back",
        body,
        [],
        [two, gn, g, gain, w_cross, cq, kv, probs, mix, b_out.reshape(1, D), acc],
        [
            ((rows // SEQ, SEQ, D), bf16),
            ((rows, D), f32),
            ((D, D), bf16),
            ((rows, D), bf16),
            (kv.shape, bf16),
            ((8, D), f32),
        ],
        [pltpu.VMEM((rows, D), bf16), pltpu.VMEM((rows, D), bf16)],
    )


def cross_weights_back(plan, gcross, gcq, gkv, gtwo, one, gain, w_query, w_kv, cin, own, other):
    rows = gcq.shape[0]
    images = rows // (2 * SEQ)
    each = other.shape[0] // images
    has = IMG_TOK - each

    def body(smem, load, out, send, extra, chunk):
        (plan,) = smem
        gone_out, gimg_out, small_out = out
        tokens, sems = extra
        flip = plan[FLIP]
        copies = []
        for p in range(images):
            at = p * IMG_TOK
            copies.append(
                pltpu.make_async_copy(
                    load(8).at[pl.ds(p * each, each), :], tokens.at[pl.ds(at + has, each), :], sems.at[2 * p]
                )
            )
            if has:
                copies.append(
                    pltpu.make_async_copy(
                        load(9).at[pl.ds(p * has, has), :], tokens.at[pl.ds(at, has), :], sems.at[2 * p + 1]
                    )
                )
        for copy in copies:
            copy.start()
        gcq, cin = load(0), load(1)
        grad_query = mm_tn(cin[...], gcq[...]).astype(bf16)
        store_blocks(chunk.first, flip, slice(D, 2 * D), grad_query)
        gone_out[...] = mm_nt(gcq[...], load(2)[...])
        gkv = load(3)
        for copy in copies:
            copy.wait()
        for j in range(2):
            cols = slice(j * D, (j + 1) * D)
            store_blocks(chunk.second, flip, cols, mm_tn(tokens[...], gkv[:, cols]).astype(bf16))
        store_blocks(chunk.first, flip, slice(0, D), load(4)[...])
        chunk.send(plan[CORE])
        one, gain, gtwo = load(5), load(6), load(7)
        gain1 = gain[1:2, :].astype(f32)
        sums = [jnp.zeros((1, D), f32) for _ in range(2)]
        for i in range(rows // SEQ):
            span = slice(i * SEQ, (i + 1) * SEQ)
            grad = gone_out[span, :]
            xhat, inv = normed(one[span, :])
            sums[0] += jnp.sum(grad * xhat, axis=0, keepdims=True)
            sums[1] += jnp.sum(grad, axis=0, keepdims=True)
            gone_out[span, :] = gtwo[span, :] + norm_back(grad, xhat, inv, gain1)
        small_out[...] = jnp.concatenate(sums + [jnp.zeros((6, D), f32)])
        send(0)
        send(2)
        gimg_out[...] = mm_nt(gkv[...], load(10)[...])

    dummy = other if own is None else own
    return staged(
        "cross_weights_back",
        body,
        [plan],
        [gcq, cin, w_query, gkv, gcross, one, gain, gtwo, other, dummy, w_kv],
        [((rows, D), f32), ((images * IMG_TOK, D), f32), ((8, D), f32)],
        [pltpu.VMEM((images * IMG_TOK, D), bf16), pltpu.SemaphoreType.DMA((2 * images,))],
        late=(8, 9),
        chunk=True,
    )


def self_scores_back(gone, qkv, probs, mix, w_self):
    rows = gone.shape[0]

    def body(smem, load, out, send, extra):
        gself, gqkv = out
        low, gmix = extra
        low[...] = load(0)[...].astype(bf16)
        gmix[...] = mm_nt(low[...], load(1)[...]).astype(bf16)
        qkv, probs = load(2), load(3)
        scaled = lane_masks(SCALE)
        plain = lane_masks(1.0)

        def attend(p):
            span = slice(p * 2 * SEQ, (p + 1) * 2 * SEQ)
            for h in range(PAIRS):
                at = 2 * HEAD_DIM * h
                q = two_heads(qkv[span, at : at + 128], scaled)
                gm = two_heads(gmix[span, at : at + 128], plain)
                k = qkv[span, D + at : D + at + 128]
                v = qkv[span, 2 * D + at : 2 * D + at + 128]
                pl_ = probs[p, h]
                pf = pl_.astype(f32)
                gp = mm_nt(gm, v)
                delta = jnp.sum(pf * gp, axis=-1, keepdims=True)
                gs = (pf * (gp - delta)).astype(bf16)
                gqkv[span, at : at + 128] = (join_heads(mm(gs, k), 2 * SEQ) * SCALE).astype(bf16)
                gqkv[span, D + at : D + at + 128] = mm_tn(gs, q).astype(bf16)
                gqkv[span, 2 * D + at : 2 * D + at + 128] = mm_tn(pl_, gm).astype(bf16)

        unrolled(rows // (2 * SEQ), attend)
        send(1)
        gself[...] = mm_tn(load(4)[...], low[...]).astype(bf16)

    return staged(
        "self_scores_back",
        body,
        [],
        [gone, w_self, qkv, probs, mix],
        [((D, D), bf16), ((rows, 3 * D), bf16)],
        [pltpu.VMEM((rows, D), bf16), pltpu.VMEM((rows, D), bf16)],
    )


def self_weights_back(plan, gself, gqkv, gone, x, attn, gain, w_qkv, small1, small2, biases):
    rows = x.shape[0]
    third = 3 * TILE

    def body(smem, load, out, send, extra, chunk):
        (plan,) = smem
        hid_out, small_out = out
        (gbase,) = extra
        flip = plan[FLIP]
        attn, gqkv = load(0), load(1)
        for j in range(3):
            grad = mm_tn(attn[...], gqkv[:, j * D : (j + 1) * D]).astype(bf16)
            if j == 0:
                store_blocks(chunk.first, flip, slice(D, 2 * D), grad)
            else:
                store_blocks(chunk.second, flip, slice((j - 1) * D, j * D), grad)
        store_blocks(chunk.first, flip, slice(0, D), load(2)[...])
        chunk.send(plan[CORE])
        gbase[...] = mm_nt(gqkv[...], load(3)[...])
        x, gone, gain = load(4), load(5), load(6)
        gain0 = gain[0:1, :].astype(f32)
        sums = [jnp.zeros((1, D), f32) for _ in range(2)]
        for i in range(rows // SEQ):
            span = slice(i * SEQ, (i + 1) * SEQ)
            grad = gbase[span, :]
            xhat, inv = normed(x[span, :].astype(f32))
            sums[0] += jnp.sum(grad * xhat, axis=0, keepdims=True)
            sums[1] += jnp.sum(grad, axis=0, keepdims=True)
            hid_out[i] = gone[span, :] + norm_back(grad, xhat, inv, gain0)
        small1, small2, bias_a, bias_b = load(7), load(8), load(9), load(10)
        small_out[...] = jnp.zeros_like(small_out)
        rows_of = [sums[0], small1[0:1, :], small2[0:1, :], sums[1], small1[1:2, :], small2[1:2, :], small2[2:3, :]]
        for i, row in enumerate(rows_of + [b[:, n * third : (n + 1) * third] for n in range(2) for b in (bias_a, bias_b)]):
            small_out[i : i + 1, :] = row

    return staged(
        "self_weights_back",
        body,
        [plan],
        [attn, gqkv, gself, w_qkv, x, gone, gain, small1, small2, *biases],
        [((rows // SEQ, SEQ, D), f32), ((16, D), f32)],
        [pltpu.VMEM((rows, D), f32)],
        chunk=True,
    )


def swap(value, axis, bit):
    size = lax.axis_size(axis)
    return lax.ppermute(value, axis, [(i, i ^ bit) for i in range(size)])


def add(a, b):
    return (a.astype(f32) + b.astype(f32)).astype(bf16)


STEPS = (("narrow", 1), ("wide", 2), ("wide", 4), ("wide", 8))
KERNEL_ADDS = 0
PARTS = {"d": {0: 2}}
ORDER = (
    "K0", "K1", "a", "K2", "b", "K3", "a", "K4", "a", "b", "c", "K5", "a+b", "a+b", "c+d", "a+b+c+d+s",
    "b+c+d+s", "a+c+d+s", "c+d+s", "a+b+d+s", "d", "b+c+d", "Fm", "Ph", "Pg", "Pi", "d", "c", "Fd", "Fc",
)


def after(token, *values):
    if token is None:
        return values[0] if len(values) == 1 else values
    tied = lax.optimization_barrier((token,) + values)[1:]
    return tied[0] if len(values) == 1 else tied


def together(token, sums):
    flat, tree = jax.tree.flatten(([s.waits() for s in sums], token))
    values, _ = jax.tree.unflatten(tree, lax.optimization_barrier(tuple(flat)))
    return [s.advance(value) for s, value in zip(sums, values)]


def add_halves(keep, got):
    half = keep.shape[0] // 2
    size = keep.shape[0] // len(got)

    def body(smem, load, out, send, extra):
        for number in (0, 1):
            for part in range(len(got)):
                i = part if number else len(got) - 1 - part
                low, high = i * size, (i + 1) * size
                first = half if number == 0 else 0
                low, high = max(low, first), min(high, first + half)
                if low < high:
                    mine = load(0)[low:high].astype(f32)
                    theirs = load(1 + i)[low - i * size : high - i * size].astype(f32)
                    out[number][low - first : high - first] = (mine + theirs).astype(bf16)
            send(number)

    shape = ((half,) + keep.shape[1:], bf16)
    return staged("add_halves", body, [], [keep] + got, [shape, shape], vmem=16)


class Chunk:
    def __init__(self, keep, *send, steps=STEPS, parts=None):
        self.keep, self.steps, self.parts = keep, steps, parts or {}
        self.back = [s for s in steps[::-1] if s[0] == "wide"]
        self.at = 0
        self.coming = [swap(part, "wide", 1) for part in send]
        self.got = []

    def waits(self):
        return [self.keep] + (self.coming if self.at == 0 else self.coming[:1])

    def advance(self, values):
        self.keep, *came = values
        self.coming = self.coming[len(came) :]
        self.got += came
        if self.coming:
            return came[0]
        got = self.got
        if self.at < len(self.steps):
            axis, bit = self.steps[self.at]
            if self.at < KERNEL_ADDS:
                out, self.keep = add_halves(self.keep, got)
            else:
                half = self.keep.shape[0] // 2
                came = jnp.concatenate(got) if len(got) > 1 else got[0]
                out = add(self.keep[half:], came[half:])
                self.keep = add(self.keep[:half], came[:half])
        else:
            first = self.at == len(self.steps)
            self.keep = out = add(self.keep, got[0]) if first else jnp.concatenate([self.keep] + got)
            spot = self.at - len(self.steps)
            axis, bit = self.back[spot] if spot < len(self.back) else ("wide", 1)
        count = self.parts.get(self.at, 1)
        size = out.shape[0] // count
        self.coming = [swap(out[i * size : (i + 1) * size], axis, bit) for i in range(count)]
        self.at += 1
        self.got = []
        return out

    def done(self, token):
        return after(token, self.keep, *self.coming)


class Small:
    def __init__(self, value):
        self.keep = value
        self.steps = (("wide", 1),) + STEPS
        self.at = 0
        self.got = swap(value, *self.steps[0])

    def waits(self):
        return [self.keep, self.got]

    def advance(self, values):
        self.keep = values[0] + values[1]
        self.at += 1
        if self.at < len(self.steps):
            self.got = swap(self.keep, *self.steps[self.at])
        return self.keep


class Away:
    def __init__(self, value, finish):
        self.got, self.finish = swap(value, "narrow", 1), finish

    def waits(self):
        return [self.got]

    def advance(self, values):
        self.out = self.finish(values[0])
        return self.out


def load_piece(plan, mine, theirs, half, index, store):
    slot = index ^ (plan[FLIP] % 8)
    core = plan[CORE]

    @pl.when(core == half)
    def _():
        store(mine[slot].astype(f32))

    @pl.when(core != half)
    def _():
        store(theirs[slot].astype(f32))


def finish_columns_kernel(cuts, plan, mine, theirs, *outs):
    for w in range(8):
        for half in range(2):

            def store(value, half=half, w=w):
                for number, src, dst, width in cuts[half]:
                    outs[number][w * BLOCK : (w + 1) * BLOCK, dst : dst + width] = value[:, src : src + width]

            load_piece(plan, mine, theirs, half, w, store)


def finish_columns(plan, pieces, cuts, widths, name):
    return pl.pallas_call(
        functools.partial(finish_columns_kernel, cuts),
        out_shape=[sds((8 * BLOCK, width), f32) for width in widths],
        in_specs=[SM, VM, VM],
        out_specs=[VM] * len(widths),
        compiler_params=params(24),
        cost_estimate=cost(0, 8e6),
        name=name,
    )(plan, *pieces)


def finish_mlp_kernel(plan, mine_a, theirs_a, mine_b, theirs_b, grad_in, grad_out):
    for call, mine, theirs in ((0, mine_a, theirs_a), (1, mine_b, theirs_b)):
        for w in range(8):

            def first(value, w=w, call=call):
                rows = slice(w * BLOCK, (w + 1) * BLOCK)
                for n in range(2):
                    dst = n * 6 * TILE + call * 3 * TILE
                    grad_in[rows, dst : dst + 3 * TILE] = value[:, n * D : (n + 1) * D]

            def second(value, w=w, call=call):
                for j in range(3):
                    for half in range(2):
                        dst = (3 * call + j) * TILE + w * 32 + half * 16
                        grad_out[dst : dst + 16, :] = value[j * 16 : (j + 1) * 16, half * D : (half + 1) * D]

            load_piece(plan, mine, theirs, 0, w, first)
            load_piece(plan, mine, theirs, 1, w, second)


def finish_mlp(plan, a, b):
    return pl.pallas_call(
        finish_mlp_kernel,
        out_shape=[sds((8 * BLOCK, FF), f32), sds((FF // 2, D), f32)],
        in_specs=[SM] + [VM] * 4,
        out_specs=[VM] * 2,
        compiler_params=params(40),
        cost_estimate=cost(0, 16e6),
        name="finish_mlp",
    )(plan, *a, *b)


def plain_sum(value):
    shard = lax.psum_scatter(value, "narrow", scatter_dimension=0, tiled=True)
    return lax.psum(shard, "wide").astype(f32)


def plain_sums(core, chunks):
    whole = []
    for keep, *send in chunks:
        send = jnp.concatenate(send)
        first = jnp.where(core == 0, keep, send)
        second = jnp.where(core == 0, send, keep)
        whole.append((first.reshape(D, WIDE_COLS), second))
    grad_in = jnp.stack([whole[0][0].reshape(D, 2, 3 * TILE), whole[1][0].reshape(D, 2, 3 * TILE)], axis=2)
    grad_out = jnp.stack([whole[0][1], whole[1][1]]).reshape(2, 2, 8, 3, 16, 2, D)
    grad_out = grad_out.transpose(1, 0, 3, 2, 5, 4, 6).reshape(FF, D)
    crosses, keys = whole[2][0], whole[2][1].reshape(D, WIDE_COLS)
    front_half, back_half = whole[3][0], whole[3][1].reshape(D, WIDE_COLS)
    return [
        plain_sum(v)
        for v in (
            jnp.concatenate([front_half[:, D:], back_half], axis=1),
            front_half[:, :D],
            crosses[:, D:],
            keys,
            crosses[:, :D],
            grad_in.reshape(D, FF),
            grad_out,
        )
    ]


def local(
    hidden_in, image_tokens, image_group, caption_len, norm_gain, norm_bias, self_qkv, self_out, cross_query,
    cross_kv, cross_out, mlp_in, mlp_bias_in, mlp_out, mlp_bias_out, out_grad,
):
    narrow = lax.axis_size("narrow")
    wide = lax.axis_size("wide")
    images, toks, _ = image_tokens.shape
    mine = images // narrow
    caps = 2 * mine
    rows = caps * SEQ
    n_at, w_at = lax.axis_index("narrow"), lax.axis_index("wide")
    fast = narrow == 2 and wide == 16
    core = w_at % 2
    if fast:
        flip = n_at * 8 + (w_at // 2) % 2 * 4 + (w_at // 4) % 2 * 2 + (w_at // 8) % 2
    else:
        flip = jnp.zeros_like(n_at)
    pos = jnp.stack([n_at, w_at * images, flip, core]).astype(jnp.int32)
    plan = make_plan(narrow, images, image_group, caption_len, pos)
    if narrow == 2:
        own, away = pick_tokens(plan, image_tokens, mine)
        got = swap(away, "narrow", 1)
        own = own.reshape(mine * toks, D)
        other = got.reshape(mine * toks, D)
    else:
        every = lax.all_gather(image_tokens, "narrow")
        first = n_at * mine
        tokens = lax.dynamic_slice_in_dim(every, first, mine, 1).transpose(1, 0, 2, 3)
        own, other = None, tokens.reshape(mine * IMG_TOK, D)
    x, attn, qkv, self_probs, self_mix, one, cin, cq, kv_own = front(
        rows, plan, hidden_in, out_grad, norm_gain, norm_bias, self_qkv, self_out, cross_query, own, cross_kv
    )
    kv, cross_probs, cross_mix, two, min_, g = cross(
        plan, kv_own, other, cq, one, norm_gain, norm_bias, cross_kv, cross_out, out_grad
    )
    state = {}
    token = min_

    def first_half(tie):
        acc, gn, bias, *chunk = mlp(0, plan, min_, g, None, None, mlp_in, mlp_bias_in, mlp_out)
        state.update(acc=acc, gn=gn, bias0=bias, a=chunk)
        return bias

    def second_half(tie):
        acc, gn = tie(state["acc"], state["gn"])
        acc, gn, bias, *chunk = mlp(1, plan, min_, g, acc, gn, mlp_in, mlp_bias_in, mlp_out)
        state.update(acc=acc, gn=gn, bias1=bias, b=chunk)
        return bias

    def cross_one(tie):
        acc, gn = tie(state["acc"], state["gn"])
        hidden_out, gtwo, gcross, gcq, gkv, small = cross_scores_back(
            acc, gn, two, g, norm_gain, mlp_bias_out, cross_out, cross_mix, cross_probs, kv, cq
        )
        state.update(hidden_out=hidden_out, gtwo=gtwo, gcross=gcross, gcq=gcq, gkv=gkv, small2=small)
        return small

    def cross_two(tie):
        gcq, gkv = tie(state["gcq"], state["gkv"])
        gone, gimg, small, *chunk = cross_weights_back(
            plan, state["gcross"], gcq, gkv, state["gtwo"], one, norm_gain, cross_query, cross_kv, cin, own, other
        )
        state.update(gone=gone, gimg=gimg, small1=small, c=chunk)
        return small

    def self_one(tie):
        gone, low_ = tie(state["gone"], self_mix)
        gself, gqkv = self_scores_back(gone, qkv, self_probs, low_, self_out)
        state.update(gself=gself, gqkv=gqkv)
        return gself

    def self_two(tie):
        gself, gqkv = tie(state["gself"], state["gqkv"])
        grad_hidden, small, *chunk = self_weights_back(
            plan, gself, gqkv, state["gone"], x, attn, norm_gain, self_qkv, state["small1"], state["small2"],
            (state["bias0"], state["bias1"]),
        )
        state.update(grad_hidden=grad_hidden, d=chunk, s=small)
        return small

    def place_out(got):
        return place(OUT_SRC, caps, plan, state["hidden_out"], got, bf16, "place_out")

    def place_grad(got):
        return place(OUT_SRC, caps, plan, state["grad_hidden"], got, f32, "place_grad")

    def place_image(got):
        return place(IMG_SRC, images, plan, state["gimg"].reshape(mine, IMG_TOK, D)[:, :toks], got, f32, "place_image")

    def finish_two(token):
        return finish_mlp(plan, live["a"].done(token), live["b"].done(token))

    def finish_cross(token):
        cuts = (((0, 0, 0, D), (1, D, 0, D)), ((2, 0, 0, 2 * D),))
        return finish_columns(plan, live["c"].done(token), cuts, (D, D, 2 * D), "finish_cross")

    def finish_self(token):
        cuts = (((0, 0, 0, D), (1, D, 0, D)), ((1, 0, D, 2 * D),))
        return finish_columns(plan, live["d"].done(token), cuts, (D, 3 * D), "finish_self")

    live = {}
    last = {"Fm": finish_two, "Fc": finish_cross, "Fd": finish_self}
    kernels = {
        "K0": first_half, "K1": second_half, "K2": cross_one, "K3": cross_two, "K4": self_one, "K5": self_two
    }
    if fast:
        for event in ORDER:
            if event in kernels:
                token = kernels[event](functools.partial(after, token))
                for name in "abcd":
                    if name in state:
                        live[name] = Chunk(*state.pop(name), parts=PARTS.get(name))
                if event == "K2":
                    away = state["hidden_out"].reshape(mine, 2, SEQ, D)[:, 1]
                    live["Ph"] = Away(away, place_out)
                if event == "K3":
                    away = state["gimg"].reshape(mine, IMG_TOK, D)[:, toks:].astype(bf16)
                    live["Pi"] = Away(away, place_image)
                if event == "K5":
                    away = state["grad_hidden"].reshape(mine, 2, SEQ, D)[:, 1].astype(bf16)
                    live["Pg"] = Away(away, place_grad)
                    live["s"] = Small(state.pop("s"))
            elif event in last:
                state[event] = last[event](token)
                token = state[event]
            else:
                token = together(token, [live[name] for name in event.split("+")])
        final_out, final_grad, grad_image = (live[name].out for name in ("Ph", "Pg", "Pi"))
        grad_mlp_in, grad_mlp_out = state["Fm"]
        grad_cross_out, grad_query, grad_kv = state["Fc"]
        grad_self_out, grad_qkv = state["Fd"]
        small = live["s"].keep
    else:
        for kernel in kernels.values():
            kernel(lambda *values: values)
        grad_qkv, grad_self_out, grad_query, grad_kv, grad_cross_out, grad_mlp_in, grad_mlp_out = plain_sums(
            core, [state[name] for name in "abcd"]
        )
        small = lax.psum(state["s"], ("wide", "narrow"))
        out_all = lax.all_gather(state["hidden_out"], "narrow", tiled=True)
        grad_all = lax.all_gather(state["grad_hidden"].astype(bf16), "narrow", tiled=True)
        final_out = place(OUT_SRC, caps, plan, out_all, out_all[:1], bf16, "place_out")
        final_grad = place(OUT_SRC, caps, plan, grad_all, grad_all[:1], f32, "place_grad")
        every = lax.all_gather(state["gimg"].reshape(mine, IMG_TOK, D).astype(bf16), "narrow", tiled=True)
        grad_image = lax.dynamic_slice_in_dim(every, n_at * toks, toks, 1).astype(f32)
    share = D // narrow
    columns = lax.dynamic_slice_in_dim(small[:7], n_at * share, share, 1)
    grad_bias_in = lax.dynamic_slice_in_dim(small[7:11].reshape(FF), n_at * (FF // narrow), FF // narrow, 0)
    return (
        final_out.reshape(rows, D),
        final_grad.reshape(rows, D),
        grad_image,
        columns[:3],
        columns[3:6],
        grad_qkv,
        grad_self_out,
        grad_query,
        grad_kv,
        grad_cross_out,
        grad_mlp_in,
        grad_bias_in,
        grad_mlp_out,
        columns[6],
    )


def solution(mesh):
    in_specs = (
        P("wide", None),
        P("wide", "narrow", None),
        P("wide"),
        P("wide"),
    ) + (P(),) * 11 + (P("wide", None),)
    out_specs = (
        P(("wide", "narrow"), None),
        P(("wide", "narrow"), None),
        P("wide", "narrow", None),
        P(None, "narrow"),
        P(None, "narrow"),
        P("narrow", None),
        P("narrow", None),
        P("narrow", None),
        P("narrow", None),
        P("narrow", None),
        P("narrow", None),
        P("narrow"),
        P("narrow", None),
        P("narrow"),
    )
    return jax.shard_map(local, mesh=mesh, in_specs=in_specs, out_specs=out_specs, check_vma=False)
```

```python
import functools

import jax
import jax.numpy as jnp
from jax import lax
from jax.experimental import pallas as pl
from jax.experimental.pallas import tpu as pltpu
from jax.sharding import PartitionSpec as P

D = 768
HEADS = 12
HEAD_DIM = 64
FF = 3072
SEQ = 64
IMG_TOK = 256
PAIRS = HEADS // 2
SCALE = HEAD_DIM**-0.5
BLOCK = 48
BLOCKS = D // BLOCK
WIDE_COLS = 2 * D
TILE = 256
f32 = jnp.float32
bf16 = jnp.bfloat16
VM = pl.BlockSpec(memory_space=pltpu.VMEM)
SM = pl.BlockSpec(memory_space=pltpu.SMEM)
ANY = pl.BlockSpec(memory_space=pl.ANY)
CORE_PARTS = 4
CAPS, LENS, MINE, PEER, IMG_SRC, OUT_SRC, FLIP, CORE, PLAN = 0, 8, 16, 20, 24, 32, 40, 41, 48


def mm(left, right):
    return lax.dot_general(left, right, (((1,), (0,)), ((), ())), preferred_element_type=f32)


def mm_nt(left, right):
    return lax.dot_general(left, right, (((1,), (1,)), ((), ())), preferred_element_type=f32)


def mm_tn(left, right):
    return lax.dot_general(left, right, (((0,), (0,)), ((), ())), preferred_element_type=f32)


def params(vmem=56, grid=None):
    return pltpu.CompilerParams(
        vmem_limit_bytes=vmem * 1024 * 1024,
        dimension_semantics=None if grid is None else ("arbitrary",) * grid,
    )


def cost(*_):
    return pl.CostEstimate(flops=1024, bytes_accessed=1024, transcendentals=0)


def sds(shape, dtype):
    return jax.ShapeDtypeStruct(shape, dtype)


def normed(x):
    center = x - jnp.mean(x, axis=-1, keepdims=True)
    inv = lax.rsqrt(jnp.mean(center * center, axis=-1, keepdims=True) + 1e-05)
    return center * inv, inv


def norm_back(grad, xhat, inv, gain):
    u = grad * gain
    return inv * (
        u - jnp.mean(u, axis=-1, keepdims=True) - xhat * jnp.mean(u * xhat, axis=-1, keepdims=True)
    )


def lane_masks(scale):
    lane = lax.broadcasted_iota(jnp.int32, (1, 2 * HEAD_DIM), 1)
    low = jnp.where(lane < HEAD_DIM, scale, 0.0).astype(bf16)
    high = jnp.where(lane < HEAD_DIM, 0.0, scale).astype(bf16)
    return low, high


def two_heads(x, masks):
    return jnp.concatenate([x * masks[0], x * masks[1]], axis=0)


def join_heads(x, rows):
    lane = lax.broadcasted_iota(jnp.int32, (rows, 2 * HEAD_DIM), 1)
    return jnp.where(lane < HEAD_DIM, x[:rows], x[rows:])


def plan_kernel(narrow, images, group, lens, pos, out, place, count):
    me = pos[0]
    base = pos[1]
    half = images // narrow
    caps = 2 * images
    for p in range(images):
        count[p] = 0
    for c in range(caps):
        g = group[c] - base
        n = count[g]
        place[2 * g + n] = c
        count[g] = n + 1
    for i in range(PLAN):
        out[i] = 0
    out[FLIP] = pos[2]
    out[CORE] = pos[3]
    slots = [jnp.int32(0) for _ in range(2)]
    turn = jnp.int32(0)
    for p in range(images):
        a = place[2 * p]
        b = place[2 * p + 1]
        if narrow == 2:
            both_low = b < images
            both_high = a >= images
            mixed = jnp.logical_not(jnp.logical_or(both_low, both_high))
            owner = jnp.where(both_low, 0, jnp.where(both_high, 1, turn))
            turn = jnp.where(mixed, 1 - turn, turn)
            slot = jnp.where(owner == 0, slots[0], slots[1])
            slots[0] = jnp.where(owner == 0, slots[0] + 1, slots[0])
            slots[1] = jnp.where(owner == 1, slots[1] + 1, slots[1])
            swap = jnp.logical_and(mixed, owner == 1)
            first = jnp.where(swap, b, a)
            second = jnp.where(swap, a, b)
            mine = owner == me

            @pl.when(mine)
            def _():
                out[MINE + slot] = p
                out[CAPS + 2 * slot] = first
                out[CAPS + 2 * slot + 1] = second
                out[LENS + 2 * slot] = lens[first]
                out[LENS + 2 * slot + 1] = lens[second]

            @pl.when(jnp.logical_not(mine))
            def _():
                out[PEER + slot] = p

            out[IMG_SRC + p] = jnp.where(mine, slot, half + slot)
            for k, c in ((0, first), (1, second)):

                @pl.when(c // images == me)
                def _():
                    out[OUT_SRC + c - me * images] = jnp.where(mine, 2 * slot + k, caps // 2 + slot)

        else:
            owner = p // half
            slot = p % half
            mine = owner == me
            per = caps // narrow

            @pl.when(mine)
            def _():
                out[MINE + slot] = p
                for k, c in ((0, a), (1, b)):
                    out[CAPS + 2 * slot + k] = c
                    out[LENS + 2 * slot + k] = lens[c]

            for k, c in ((0, a), (1, b)):

                @pl.when(c // per == me)
                def _():
                    out[OUT_SRC + c - me * per] = 2 * p + k


def make_plan(narrow, images, group, lens, pos):
    return pl.pallas_call(
        functools.partial(plan_kernel, narrow, images),
        out_shape=sds((PLAN,), jnp.int32),
        in_specs=[SM, SM, SM],
        out_specs=SM,
        scratch_shapes=[
            pltpu.SMEM((2 * images,), jnp.int32),
            pltpu.SMEM((images,), jnp.int32),
        ],
        compiler_params=params(4),
        name="plan",
    )(group, lens, pos)


def pick_kernel(plan, tokens_a, tokens_b, mine, peer):
    mine[...] = tokens_a[...]
    peer[...] = tokens_b[...]


def pick_tokens(plan, tokens, count):
    block = (1,) + tokens.shape[1:]
    return pl.pallas_call(
        pick_kernel,
        grid_spec=pltpu.PrefetchScalarGridSpec(
            num_scalar_prefetch=1,
            grid=(count,),
            in_specs=[
                pl.BlockSpec(block, lambda i, plan: (plan[MINE + i], 0, 0)),
                pl.BlockSpec(block, lambda i, plan: (plan[PEER + i], 0, 0)),
            ],
            out_specs=[pl.BlockSpec(block, lambda i, plan: (i, 0, 0))] * 2,
        ),
        out_shape=[sds((count,) + tokens.shape[1:], bf16)] * 2,
        compiler_params=params(8),
        name="pick",
    )(plan, tokens, tokens)


def place_kernel(offset, count, plan, own, got, out):
    have = own.shape[0]
    for i in range(count):
        src = plan[offset + i]

        @pl.when(src < have)
        def _():
            out[i] = own[jnp.minimum(src, have - 1)].astype(out.dtype)

        @pl.when(src >= have)
        def _():
            out[i] = got[jnp.maximum(src - have, 0)].astype(out.dtype)


def place(offset, count, plan, own, got, dtype, name):
    return pl.pallas_call(
        functools.partial(place_kernel, offset, count),
        out_shape=sds((count,) + own.shape[1:], dtype),
        in_specs=[SM, VM, VM],
        out_specs=VM,
        compiler_params=params(24),
        cost_estimate=cost(0, 4 * count * own.shape[1] * own.shape[2] * 2),
        name=name,
    )(plan, own, got)


WINDOW = 8


def staged(name, body, smem, ins, outs, extra=(), late=(), chunk=False, vmem=56):
    n_s, n_i, n_o, n_e = len(smem), len(ins), len(outs), len(extra)
    n_c = 1 + CORE_PARTS if chunk else 0
    staged_ins = [i for i in range(n_i) if i not in late]

    def kernel(*refs):
        refs = list(refs)
        take = lambda n: [refs.pop(0) for _ in range(n)]
        scalars, h_in, h_out = take(n_s), take(n_i), take(n_o)
        chunk_out = take(n_c)
        v_in = dict(zip(staged_ins, take(len(staged_ins))))
        v_out, more = take(n_o), take(n_e)
        staging = Staging(chunk_out, *take(3)) if chunk else None
        in_sem, out_sem = refs
        copies = {i: pltpu.make_async_copy(h_in[i], v_in[i], in_sem.at[i]) for i in staged_ins}
        started, waited, going = [], set(), []

        def ahead(count):
            for i in staged_ins:
                if count <= 0:
                    return
                if i not in started:
                    copies[i].start()
                    started.append(i)
                    count -= 1

        ahead(WINDOW)

        def load(i):
            if i in late:
                return h_in[i]
            if i not in waited:
                assert i in started
                copies[i].wait()
                waited.add(i)
                ahead(1)
            return v_in[i]

        def send(i):
            copy = pltpu.make_async_copy(v_out[i], h_out[i], out_sem.at[i])
            copy.start()
            going.append((i, copy))

        body(scalars, load, v_out, send, more, *([staging] if chunk else []))
        sent = {i for i, _ in going}
        for i in range(n_o):
            if i not in sent and outs[i] is not None:
                send(i)
        for i in staged_ins:
            load(i)
        for _, copy in going:
            copy.wait()
        if chunk:
            staging.wait()

    return pl.pallas_call(
        kernel,
        out_shape=[sds(*o) for o in outs] + [sds(*o) for o in CHUNK_OUTS[:n_c]],
        in_specs=[SM] * n_s + [ANY] * n_i,
        out_specs=[ANY] * (n_o + n_c),
        scratch_shapes=[pltpu.VMEM(ins[i].shape, ins[i].dtype) for i in staged_ins]
        + [pltpu.VMEM(*o) for o in outs]
        + list(extra)
        + (chunk_extra() if chunk else [])
        + [pltpu.SemaphoreType.DMA((max(n_i, 1),)), pltpu.SemaphoreType.DMA((max(n_o, 1),))],
        compiler_params=params(vmem),
        cost_estimate=cost(),
        name=name,
    )(*smem, *ins)


def unrolled(count, step):
    for i in range(count):
        step(i)


def front(rows, plan, hidden, out_grad, gain, bias, w_qkv, w_self, w_query, own, w_kv):
    pairs = rows // (2 * SEQ)
    kv_rows = 0 if own is None else own.shape[0]

    def body(smem, load, out, send, extra):
        (plan,) = smem
        x_out, attn_out, qkv_out, probs_out, mix_out, one_out, cin_out, cq_out, kv_out = out
        hidden = load(0)
        gain, bias = load(1), load(2)
        gain0, bias0 = gain[0:1, :].astype(f32), bias[0:1, :].astype(f32)
        gain1, bias1 = gain[1:2, :].astype(f32), bias[1:2, :].astype(f32)

        def gather(i):
            src = pl.ds(pl.multiple_of(plan[CAPS + i] * SEQ, SEQ), SEQ)
            dst = slice(i * SEQ, (i + 1) * SEQ)
            x = hidden[src, :]
            x_out[dst, :] = x
            attn_out[dst, :] = (normed(x.astype(f32))[0] * gain0 + bias0).astype(bf16)

        unrolled(rows // SEQ, gather)
        send(0)
        send(1)
        w_qkv = load(3)
        for j in range(3):
            cols = slice(j * D, (j + 1) * D)
            qkv_out[:, cols] = mm(attn_out[...], w_qkv[:, cols]).astype(bf16)
        send(2)
        masks = lane_masks(SCALE)
        row = lax.broadcasted_iota(jnp.int32, (2 * SEQ, 2 * SEQ), 0)
        col = lax.broadcasted_iota(jnp.int32, (2 * SEQ, 2 * SEQ), 1)
        causal = jnp.logical_and(col <= row, (col // SEQ) == (row // SEQ))

        def attend(p):
            span = slice(p * 2 * SEQ, (p + 1) * 2 * SEQ)
            length = jnp.where(col < SEQ, plan[LENS + 2 * p], plan[LENS + 2 * p + 1])
            allowed = jnp.logical_and(causal, (col % SEQ) < length)
            fill = jnp.where(allowed, 0.0, -1e30)
            fill = jnp.concatenate([fill, fill], axis=0)
            for h in range(PAIRS):
                at = 2 * HEAD_DIM * h
                q = two_heads(qkv_out[span, at : at + 128], masks)
                k = qkv_out[span, D + at : D + at + 128]
                v = qkv_out[span, 2 * D + at : 2 * D + at + 128]
                logits = jnp.where(fill < 0.0, fill, mm_nt(q, k))
                e = jnp.exp(logits - jnp.max(logits, axis=-1, keepdims=True))
                low = (e * (1.0 / jnp.sum(e, axis=-1, keepdims=True))).astype(bf16)
                probs_out[p, h] = low
                mix_out[span, at : at + 128] = join_heads(mm(low, v), 2 * SEQ).astype(bf16)

        unrolled(pairs, attend)
        send(3)
        send(4)
        one_out[...] = mm(mix_out[...], load(4)[...])

        def second(i):
            span = slice(i * SEQ, (i + 1) * SEQ)
            one = one_out[span, :] + x_out[span, :].astype(f32)
            one_out[span, :] = one
            cin_out[span, :] = (normed(one)[0] * gain1 + bias1).astype(bf16)

        unrolled(rows // SEQ, second)
        send(5)
        send(6)
        cq_out[...] = mm(cin_out[...], load(5)[...]).astype(bf16)
        send(7)
        if own is not None:
            for j in range(2):
                cols = slice(j * D, (j + 1) * D)
                kv_out[:, cols] = mm(load(6)[...], load(7)[:, cols]).astype(bf16)

    ins = [hidden, gain, bias, w_qkv, w_self, w_query] + ([] if own is None else [own, w_kv])
    return staged(
        "front",
        body,
        [plan],
        ins,
        [
            ((rows, D), bf16),
            ((rows, D), bf16),
            ((rows, 3 * D), bf16),
            ((pairs, PAIRS, 4 * SEQ, 2 * SEQ), bf16),
            ((rows, D), bf16),
            ((rows, D), f32),
            ((rows, D), bf16),
            ((rows, D), bf16),
            ((max(kv_rows, 16), 2 * D), bf16),
        ],
    )


def cross(plan, kv_own, tokens, cq, one, gain, bias, w_kv, w_cross, out_grad):
    rows = cq.shape[0]
    images = rows // (2 * SEQ)
    each = tokens.shape[0] // images
    has = IMG_TOK - each

    def body(smem, load, out, send, extra):
        (plan,) = smem
        kv_out, probs_out, mix_out, two_out, min_out, g_out = out
        raw, grads_in = extra
        gather = [
            pltpu.make_async_copy(
                load(8).at[pl.ds(pl.multiple_of(plan[CAPS + i] * SEQ, SEQ), SEQ), :],
                g_out.at[pl.ds(i * SEQ, SEQ), :],
                grads_in.at[i],
            )
            for i in range(rows // SEQ)
        ]
        for copy in gather:
            copy.start()
        tokens, w_kv = load(0), load(1)
        for j in range(2):
            cols = slice(j * D, (j + 1) * D)
            raw[:, cols] = mm(tokens[...], w_kv[:, cols]).astype(bf16)
        for p in range(images):
            kv_out[p * IMG_TOK + has : (p + 1) * IMG_TOK, :] = raw[p * each : (p + 1) * each, :]
            if has:
                kv_out[p * IMG_TOK : p * IMG_TOK + has, :] = load(2)[p * has : (p + 1) * has, :]
        send(0)
        cq = load(3)
        masks = lane_masks(SCALE)

        def attend(p):
            span = slice(p * 2 * SEQ, (p + 1) * 2 * SEQ)
            toks = slice(p * IMG_TOK, (p + 1) * IMG_TOK)
            for h in range(PAIRS):
                at = 2 * HEAD_DIM * h
                q = two_heads(cq[span, at : at + 128], masks)
                logits = mm_nt(q, kv_out[toks, at : at + 128])
                e = jnp.exp(logits - jnp.max(logits, axis=-1, keepdims=True))
                low = (e * (1.0 / jnp.sum(e, axis=-1, keepdims=True))).astype(bf16)
                probs_out[p, h] = low
                mix = mm(low, kv_out[toks, D + at : D + at + 128])
                mix_out[span, at : at + 128] = join_heads(mix, 2 * SEQ).astype(bf16)

        unrolled(images, attend)
        send(1)
        send(2)
        two_out[...] = mm(mix_out[...], load(4)[...])
        one, gain, bias = load(5), load(6), load(7)
        gain2, bias2 = gain[2:3, :].astype(f32), bias[2:3, :].astype(f32)

        def second(i):
            span = slice(i * SEQ, (i + 1) * SEQ)
            two = two_out[span, :] + one[span, :]
            two_out[span, :] = two
            min_out[span, :] = (normed(two)[0] * gain2 + bias2).astype(bf16)

        unrolled(rows // SEQ, second)
        for copy in gather:
            copy.wait()

    return staged(
        "cross",
        body,
        [plan],
        [tokens, w_kv, kv_own, cq, w_cross, one, gain, bias, out_grad],
        [
            ((images * IMG_TOK, 2 * D), bf16),
            ((images, PAIRS, 4 * SEQ, IMG_TOK), bf16),
            ((rows, D), bf16),
            ((rows, D), f32),
            ((rows, D), bf16),
            ((rows, D), bf16),
        ],
        [pltpu.VMEM((tokens.shape[0], 2 * D), bf16), pltpu.SemaphoreType.DMA((rows // SEQ,))],
        late=(8,),
    )


CHUNK_OUTS = [((BLOCKS, BLOCK, WIDE_COLS), bf16)] + [((BLOCKS // CORE_PARTS, BLOCK, WIDE_COLS), bf16)] * CORE_PARTS


def chunk_extra():
    return [
        pltpu.VMEM((BLOCKS, BLOCK, WIDE_COLS), bf16),
        pltpu.VMEM((BLOCKS, BLOCK, WIDE_COLS), bf16),
        pltpu.SemaphoreType.DMA((1 + CORE_PARTS,)),
    ]


class Staging:
    def __init__(self, outs, first, second, sems):
        self.keep, *self.parts = outs
        self.first, self.second, self.sems = first, second, sems

    def copies(self, kept, sent):
        size = BLOCKS // CORE_PARTS
        return [pltpu.make_async_copy(kept, self.keep, self.sems.at[CORE_PARTS])] + [
            pltpu.make_async_copy(sent.at[pl.ds(i * size, size)], self.parts[i], self.sems.at[i])
            for i in range(CORE_PARTS)
        ]

    def send(self, core):
        @pl.when(core == 0)
        def _():
            for copy in self.copies(self.first, self.second):
                copy.start()

        @pl.when(core != 0)
        def _():
            for copy in self.copies(self.second, self.first):
                copy.start()

    def wait(self):
        for copy in self.copies(self.first, self.second):
            copy.wait()


def store_blocks(ref, flip, cols, value):
    for b in range(BLOCKS):
        ref[b ^ flip, :, cols] = value[b * BLOCK : (b + 1) * BLOCK, :]


def mlp(call, plan, min_, g, acc, gn, w_in, b_in, w_out):
    rows = g.shape[0]
    tiles = [k + 3 * (k // 3) + 3 * call for k in range(6)]
    carried = acc is not None

    def kernel(*refs):
        refs = list(refs)
        take = lambda n: [refs.pop(0) for _ in range(n)]
        (plan,) = take(1)
        h_min, h_g, h_bias, h_in, h_out = take(5)
        h_acc, h_gn = take(2) if carried else (None, None)
        o_acc, o_gn, o_bias, o_keep = take(4)
        o_parts = take(CORE_PARTS)
        v_min, v_g, v_bias, v_in, v_out, v_acc, v_gn, gbias, act, low, min_t, first, second, chunk_sem, sems = refs
        flip = plan[FLIP]
        staging = Staging([o_keep] + o_parts, first, second, chunk_sem)
        copies = [
            pltpu.make_async_copy(h_min, v_min, sems.at[0]),
            pltpu.make_async_copy(h_bias, v_bias, sems.at[1]),
        ]
        for k, t in enumerate(tiles):
            mine, there = pl.ds(k * TILE, TILE), pl.ds(t * TILE, TILE)
            copies.append(pltpu.make_async_copy(h_in.at[:, there], v_in.at[:, mine], sems.at[2 + 2 * k]))
            copies.append(pltpu.make_async_copy(h_out.at[there, :], v_out.at[mine, :], sems.at[3 + 2 * k]))
        copies.insert(3, pltpu.make_async_copy(h_g, v_g, sems.at[14]))
        if carried:
            copies.append(pltpu.make_async_copy(h_acc, v_acc, sems.at[15]))
            copies.append(pltpu.make_async_copy(h_gn, v_gn, sems.at[16]))
        queue = list(copies)
        for _ in range(6):
            queue.pop(0).start()

        def wait(count):
            for _ in range(count):
                copies.pop(0).wait()
                if queue:
                    queue.pop(0).start()

        wait(2)
        min_t[...] = v_min[...].T
        for k, t in enumerate(tiles):
            wait(3 if k == 0 else 2)
            cols = slice(k * TILE, (k + 1) * TILE)
            pre = mm(v_min[...], v_in[:, cols]) + v_bias[:, t * TILE : (t + 1) * TILE].astype(f32)
            phi = 0.5 + 0.5 * lax.erf(pre * (2.0**-0.5))
            act[:, cols] = (pre * phi).astype(bf16)
            slope = phi + pre * jnp.exp(-0.5 * pre * pre) * 0.3989422804014327
            grad_pre = slope * mm_nt(v_g[...], v_out[cols, :])
            gbias[:, cols] = jnp.sum(grad_pre, axis=0, keepdims=True)
            low[:, cols] = grad_pre.astype(bf16)
            grad_in = mm(min_t[...], low[:, cols]).astype(bf16)
            grad_out = mm_tn(act[:, cols], v_g[...]).astype(bf16)
            store_blocks(first, flip, cols, grad_in)
            spot = slice((k % 3) * 16, (k % 3 + 1) * 16)
            for w in range(8):
                slot = ((k // 3) * 8 + w) ^ flip
                second[slot, spot, 0:D] = grad_out[w * 32 : w * 32 + 16, :]
                second[slot, spot, D : 2 * D] = grad_out[w * 32 + 16 : w * 32 + 32, :]
        staging.send(plan[CORE])
        wait(len(copies))
        if carried:
            v_gn[...] += mm_nt(low[...], v_in[...])
        else:
            v_gn[...] = mm_nt(low[...], v_in[...])
        back = pltpu.make_async_copy(v_gn, o_gn, sems.at[17])
        back.start()
        if carried:
            v_acc[...] += mm(act[...], v_out[...])
        else:
            v_acc[...] = mm(act[...], v_out[...])
        more = [
            pltpu.make_async_copy(v_acc, o_acc, sems.at[18]),
            pltpu.make_async_copy(gbias, o_bias, sems.at[19]),
        ]
        for copy in more:
            copy.start()
        for copy in [back] + more:
            copy.wait()
        staging.wait()

    half = 6 * TILE
    ins = [min_, g, b_in.reshape(1, FF), w_in, w_out] + ([acc, gn] if carried else [])
    return pl.pallas_call(
        kernel,
        out_shape=[sds((rows, D), f32), sds((rows, D), f32), sds((1, half), f32)] + [sds(*o) for o in CHUNK_OUTS],
        in_specs=[SM] + [ANY] * len(ins),
        out_specs=[ANY] * (4 + CORE_PARTS),
        scratch_shapes=[
            pltpu.VMEM((rows, D), bf16),
            pltpu.VMEM((rows, D), bf16),
            pltpu.VMEM((1, FF), bf16),
            pltpu.VMEM((D, half), bf16),
            pltpu.VMEM((half, D), bf16),
            pltpu.VMEM((rows, D), f32),
            pltpu.VMEM((rows, D), f32),
            pltpu.VMEM((1, half), f32),
            pltpu.VMEM((rows, half), bf16),
            pltpu.VMEM((rows, half), bf16),
            pltpu.VMEM((D, rows), bf16),
        ]
        + chunk_extra()
        + [pltpu.SemaphoreType.DMA((20,))],
        compiler_params=params(),
        cost_estimate=cost(),
        name="mlp",
    )(plan, *ins)


def cross_scores_back(acc, gn, two, g, gain, b_out, w_cross, mix, probs, kv, cq):
    rows = cq.shape[0]
    images = rows // (2 * SEQ)

    def body(smem, load, out, send, extra):
        hid_out, gtwo, gcross, gcq, gkv, small_out = out
        low, gmix = extra
        two, gn, g, gain = load(0), load(1), load(2), load(3)
        gain2 = gain[2:3, :].astype(f32)
        sums = [jnp.zeros((1, D), f32) for _ in range(3)]
        for i in range(rows // SEQ):
            span = slice(i * SEQ, (i + 1) * SEQ)
            up = g[span, :].astype(f32)
            grad = gn[span, :]
            xhat, inv = normed(two[span, :])
            sums[0] += jnp.sum(grad * xhat, axis=0, keepdims=True)
            sums[1] += jnp.sum(grad, axis=0, keepdims=True)
            sums[2] += jnp.sum(up, axis=0, keepdims=True)
            total = up + norm_back(grad, xhat, inv, gain2)
            gtwo[span, :] = total
            low[span, :] = total.astype(bf16)
        small_out[...] = jnp.concatenate(sums + [jnp.zeros((5, D), f32)])
        send(1)
        send(5)
        gmix[...] = mm_nt(low[...], load(4)[...]).astype(bf16)
        cq, kv, probs = load(5), load(6), load(7)
        scaled = lane_masks(SCALE)
        plain = lane_masks(1.0)

        def attend(p):
            span = slice(p * 2 * SEQ, (p + 1) * 2 * SEQ)
            toks = slice(p * IMG_TOK, (p + 1) * IMG_TOK)
            for h in range(PAIRS):
                at = 2 * HEAD_DIM * h
                q = two_heads(cq[span, at : at + 128], scaled)
                gm = two_heads(gmix[span, at : at + 128], plain)
                k = kv[toks, at : at + 128]
                v = kv[toks, D + at : D + at + 128]
                pl_ = probs[p, h]
                pf = pl_.astype(f32)
                gp = mm_nt(gm, v)
                delta = jnp.sum(pf * gp, axis=-1, keepdims=True)
                gs = (pf * (gp - delta)).astype(bf16)
                gcq[span, at : at + 128] = (join_heads(mm(gs, k), 2 * SEQ) * SCALE).astype(bf16)
                gkv[toks, at : at + 128] = mm_tn(gs, q).astype(bf16)
                gkv[toks, D + at : D + at + 128] = mm_tn(pl_, gm).astype(bf16)

        unrolled(images, attend)
        send(3)
        send(4)
        gcross[...] = mm_tn(load(8)[...], low[...]).astype(bf16)
        send(2)
        bias_out = load(9)[...].astype(f32)
        acc = load(10)
        for i in range(rows // SEQ):
            span = slice(i * SEQ, (i + 1) * SEQ)
            hid_out[i] = (two[span, :] + (acc[span, :] + bias_out)).astype(bf16)

    return staged(
        "cross_scores_back",
        body,
        [],
        [two, gn, g, gain, w_cross, cq, kv, probs, mix, b_out.reshape(1, D), acc],
        [
            ((rows // SEQ, SEQ, D), bf16),
            ((rows, D), f32),
            ((D, D), bf16),
            ((rows, D), bf16),
            (kv.shape, bf16),
            ((8, D), f32),
        ],
        [pltpu.VMEM((rows, D), bf16), pltpu.VMEM((rows, D), bf16)],
    )


def cross_weights_back(plan, gcross, gcq, gkv, gtwo, one, gain, w_query, w_kv, cin, own, other):
    rows = gcq.shape[0]
    images = rows // (2 * SEQ)
    each = other.shape[0] // images
    has = IMG_TOK - each

    def body(smem, load, out, send, extra, chunk):
        (plan,) = smem
        gone_out, gimg_out, small_out = out
        tokens, sems = extra
        flip = plan[FLIP]
        copies = []
        for p in range(images):
            at = p * IMG_TOK
            copies.append(
                pltpu.make_async_copy(
                    load(8).at[pl.ds(p * each, each), :], tokens.at[pl.ds(at + has, each), :], sems.at[2 * p]
                )
            )
            if has:
                copies.append(
                    pltpu.make_async_copy(
                        load(9).at[pl.ds(p * has, has), :], tokens.at[pl.ds(at, has), :], sems.at[2 * p + 1]
                    )
                )
        for copy in copies:
            copy.start()
        gcq, cin = load(0), load(1)
        grad_query = mm_tn(cin[...], gcq[...]).astype(bf16)
        store_blocks(chunk.first, flip, slice(D, 2 * D), grad_query)
        gone_out[...] = mm_nt(gcq[...], load(2)[...])
        gkv = load(3)
        for copy in copies:
            copy.wait()
        for j in range(2):
            cols = slice(j * D, (j + 1) * D)
            store_blocks(chunk.second, flip, cols, mm_tn(tokens[...], gkv[:, cols]).astype(bf16))
        store_blocks(chunk.first, flip, slice(0, D), load(4)[...])
        chunk.send(plan[CORE])
        one, gain, gtwo = load(5), load(6), load(7)
        gain1 = gain[1:2, :].astype(f32)
        sums = [jnp.zeros((1, D), f32) for _ in range(2)]
        for i in range(rows // SEQ):
            span = slice(i * SEQ, (i + 1) * SEQ)
            grad = gone_out[span, :]
            xhat, inv = normed(one[span, :])
            sums[0] += jnp.sum(grad * xhat, axis=0, keepdims=True)
            sums[1] += jnp.sum(grad, axis=0, keepdims=True)
            gone_out[span, :] = gtwo[span, :] + norm_back(grad, xhat, inv, gain1)
        small_out[...] = jnp.concatenate(sums + [jnp.zeros((6, D), f32)])
        send(0)
        send(2)
        gimg_out[...] = mm_nt(gkv[...], load(10)[...])

    dummy = other if own is None else own
    return staged(
        "cross_weights_back",
        body,
        [plan],
        [gcq, cin, w_query, gkv, gcross, one, gain, gtwo, other, dummy, w_kv],
        [((rows, D), f32), ((images * IMG_TOK, D), f32), ((8, D), f32)],
        [pltpu.VMEM((images * IMG_TOK, D), bf16), pltpu.SemaphoreType.DMA((2 * images,))],
        late=(8, 9),
        chunk=True,
    )


def self_scores_back(gone, qkv, probs, mix, w_self):
    rows = gone.shape[0]

    def body(smem, load, out, send, extra):
        gself, gqkv = out
        low, gmix = extra
        low[...] = load(0)[...].astype(bf16)
        gmix[...] = mm_nt(low[...], load(1)[...]).astype(bf16)
        qkv, probs = load(2), load(3)
        scaled = lane_masks(SCALE)
        plain = lane_masks(1.0)

        def attend(p):
            span = slice(p * 2 * SEQ, (p + 1) * 2 * SEQ)
            for h in range(PAIRS):
                at = 2 * HEAD_DIM * h
                q = two_heads(qkv[span, at : at + 128], scaled)
                gm = two_heads(gmix[span, at : at + 128], plain)
                k = qkv[span, D + at : D + at + 128]
                v = qkv[span, 2 * D + at : 2 * D + at + 128]
                pl_ = probs[p, h]
                pf = pl_.astype(f32)
                gp = mm_nt(gm, v)
                delta = jnp.sum(pf * gp, axis=-1, keepdims=True)
                gs = (pf * (gp - delta)).astype(bf16)
                gqkv[span, at : at + 128] = (join_heads(mm(gs, k), 2 * SEQ) * SCALE).astype(bf16)
                gqkv[span, D + at : D + at + 128] = mm_tn(gs, q).astype(bf16)
                gqkv[span, 2 * D + at : 2 * D + at + 128] = mm_tn(pl_, gm).astype(bf16)

        unrolled(rows // (2 * SEQ), attend)
        send(1)
        gself[...] = mm_tn(load(4)[...], low[...]).astype(bf16)

    return staged(
        "self_scores_back",
        body,
        [],
        [gone, w_self, qkv, probs, mix],
        [((D, D), bf16), ((rows, 3 * D), bf16)],
        [pltpu.VMEM((rows, D), bf16), pltpu.VMEM((rows, D), bf16)],
    )


def self_weights_back(plan, gself, gqkv, gone, x, attn, gain, w_qkv, small1, small2, biases):
    rows = x.shape[0]
    third = 3 * TILE

    def body(smem, load, out, send, extra, chunk):
        (plan,) = smem
        hid_out, small_out = out
        (gbase,) = extra
        flip = plan[FLIP]
        attn, gqkv = load(0), load(1)
        for j in range(3):
            grad = mm_tn(attn[...], gqkv[:, j * D : (j + 1) * D]).astype(bf16)
            if j == 0:
                store_blocks(chunk.first, flip, slice(D, 2 * D), grad)
            else:
                store_blocks(chunk.second, flip, slice((j - 1) * D, j * D), grad)
        store_blocks(chunk.first, flip, slice(0, D), load(2)[...])
        chunk.send(plan[CORE])
        gbase[...] = mm_nt(gqkv[...], load(3)[...])
        x, gone, gain = load(4), load(5), load(6)
        gain0 = gain[0:1, :].astype(f32)
        sums = [jnp.zeros((1, D), f32) for _ in range(2)]
        for i in range(rows // SEQ):
            span = slice(i * SEQ, (i + 1) * SEQ)
            grad = gbase[span, :]
            xhat, inv = normed(x[span, :].astype(f32))
            sums[0] += jnp.sum(grad * xhat, axis=0, keepdims=True)
            sums[1] += jnp.sum(grad, axis=0, keepdims=True)
            hid_out[i] = gone[span, :] + norm_back(grad, xhat, inv, gain0)
        small1, small2, bias_a, bias_b = load(7), load(8), load(9), load(10)
        small_out[...] = jnp.zeros_like(small_out)
        rows_of = [sums[0], small1[0:1, :], small2[0:1, :], sums[1], small1[1:2, :], small2[1:2, :], small2[2:3, :]]
        for i, row in enumerate(rows_of + [b[:, n * third : (n + 1) * third] for n in range(2) for b in (bias_a, bias_b)]):
            small_out[i : i + 1, :] = row

    return staged(
        "self_weights_back",
        body,
        [plan],
        [attn, gqkv, gself, w_qkv, x, gone, gain, small1, small2, *biases],
        [((rows // SEQ, SEQ, D), f32), ((16, D), f32)],
        [pltpu.VMEM((rows, D), f32)],
        chunk=True,
    )


def swap(value, axis, bit):
    size = lax.axis_size(axis)
    return lax.ppermute(value, axis, [(i, i ^ bit) for i in range(size)])


def add(a, b):
    return (a.astype(f32) + b.astype(f32)).astype(bf16)


STEPS = (("narrow", 1), ("wide", 2), ("wide", 4), ("wide", 8))
KERNEL_ADDS = 0
PARTS = {"d": {0: 2}}
ORDER = (
    "K0", "K1", "a", "K2", "b", "K3", "a", "K4", "a", "b", "c", "K5", "a+b", "a+b", "c+d", "a+b+c+d+s",
    "b+c+d+s", "a+c+d+s", "c+d+s", "a+b+d+s", "d", "b+c+d", "Fm", "Ph", "Pg", "Pi", "d", "c", "Fd", "Fc",
)


def after(token, *values):
    if token is None:
        return values[0] if len(values) == 1 else values
    tied = lax.optimization_barrier((token,) + values)[1:]
    return tied[0] if len(values) == 1 else tied


def together(token, sums):
    flat, tree = jax.tree.flatten(([s.waits() for s in sums], token))
    values, _ = jax.tree.unflatten(tree, lax.optimization_barrier(tuple(flat)))
    return [s.advance(value) for s, value in zip(sums, values)]


def add_halves(keep, got):
    half = keep.shape[0] // 2
    size = keep.shape[0] // len(got)

    def body(smem, load, out, send, extra):
        for number in (0, 1):
            for part in range(len(got)):
                i = part if number else len(got) - 1 - part
                low, high = i * size, (i + 1) * size
                first = half if number == 0 else 0
                low, high = max(low, first), min(high, first + half)
                if low < high:
                    mine = load(0)[low:high].astype(f32)
                    theirs = load(1 + i)[low - i * size : high - i * size].astype(f32)
                    out[number][low - first : high - first] = (mine + theirs).astype(bf16)
            send(number)

    shape = ((half,) + keep.shape[1:], bf16)
    return staged("add_halves", body, [], [keep] + got, [shape, shape], vmem=16)


class Chunk:
    def __init__(self, keep, *send, steps=STEPS, parts=None):
        self.keep, self.steps, self.parts = keep, steps, parts or {}
        self.back = [s for s in steps[::-1] if s[0] == "wide"]
        self.at = 0
        self.coming = [swap(part, "wide", 1) for part in send]
        self.got = []

    def waits(self):
        return [self.keep] + (self.coming if self.at == 0 else self.coming[:1])

    def advance(self, values):
        self.keep, *came = values
        self.coming = self.coming[len(came) :]
        self.got += came
        if self.coming:
            return came[0]
        got = self.got
        if self.at < len(self.steps):
            axis, bit = self.steps[self.at]
            if self.at < KERNEL_ADDS:
                out, self.keep = add_halves(self.keep, got)
            else:
                half = self.keep.shape[0] // 2
                came = jnp.concatenate(got) if len(got) > 1 else got[0]
                out = add(self.keep[half:], came[half:])
                self.keep = add(self.keep[:half], came[:half])
        else:
            first = self.at == len(self.steps)
            self.keep = out = add(self.keep, got[0]) if first else jnp.concatenate([self.keep] + got)
            spot = self.at - len(self.steps)
            axis, bit = self.back[spot] if spot < len(self.back) else ("wide", 1)
        count = self.parts.get(self.at, 1)
        size = out.shape[0] // count
        self.coming = [swap(out[i * size : (i + 1) * size], axis, bit) for i in range(count)]
        self.at += 1
        self.got = []
        return out

    def done(self, token):
        return after(token, self.keep, *self.coming)


class Small:
    def __init__(self, value):
        self.keep = value
        self.steps = (("wide", 1),) + STEPS
        self.at = 0
        self.got = swap(value, *self.steps[0])

    def waits(self):
        return [self.keep, self.got]

    def advance(self, values):
        self.keep = values[0] + values[1]
        self.at += 1
        if self.at < len(self.steps):
            self.got = swap(self.keep, *self.steps[self.at])
        return self.keep


class Away:
    def __init__(self, value, finish):
        self.got, self.finish = swap(value, "narrow", 1), finish

    def waits(self):
        return [self.got]

    def advance(self, values):
        self.out = self.finish(values[0])
        return self.out


def load_piece(plan, mine, theirs, half, index, store):
    slot = index ^ (plan[FLIP] % 8)
    core = plan[CORE]

    @pl.when(core == half)
    def _():
        store(mine[slot].astype(f32))

    @pl.when(core != half)
    def _():
        store(theirs[slot].astype(f32))


def finish_columns_kernel(cuts, plan, mine, theirs, *outs):
    for w in range(8):
        for half in range(2):

            def store(value, half=half, w=w):
                for number, src, dst, width in cuts[half]:
                    outs[number][w * BLOCK : (w + 1) * BLOCK, dst : dst + width] = value[:, src : src + width]

            load_piece(plan, mine, theirs, half, w, store)


def finish_columns(plan, pieces, cuts, widths, name):
    return pl.pallas_call(
        functools.partial(finish_columns_kernel, cuts),
        out_shape=[sds((8 * BLOCK, width), f32) for width in widths],
        in_specs=[SM, VM, VM],
        out_specs=[VM] * len(widths),
        compiler_params=params(24),
        cost_estimate=cost(0, 8e6),
        name=name,
    )(plan, *pieces)


def finish_mlp_kernel(plan, mine_a, theirs_a, mine_b, theirs_b, grad_in, grad_out):
    for call, mine, theirs in ((0, mine_a, theirs_a), (1, mine_b, theirs_b)):
        for w in range(8):

            def first(value, w=w, call=call):
                rows = slice(w * BLOCK, (w + 1) * BLOCK)
                for n in range(2):
                    dst = n * 6 * TILE + call * 3 * TILE
                    grad_in[rows, dst : dst + 3 * TILE] = value[:, n * D : (n + 1) * D]

            def second(value, w=w, call=call):
                for j in range(3):
                    for half in range(2):
                        dst = (3 * call + j) * TILE + w * 32 + half * 16
                        grad_out[dst : dst + 16, :] = value[j * 16 : (j + 1) * 16, half * D : (half + 1) * D]

            load_piece(plan, mine, theirs, 0, w, first)
            load_piece(plan, mine, theirs, 1, w, second)


def finish_mlp(plan, a, b):
    return pl.pallas_call(
        finish_mlp_kernel,
        out_shape=[sds((8 * BLOCK, FF), f32), sds((FF // 2, D), f32)],
        in_specs=[SM] + [VM] * 4,
        out_specs=[VM] * 2,
        compiler_params=params(40),
        cost_estimate=cost(0, 16e6),
        name="finish_mlp",
    )(plan, *a, *b)


def plain_sum(value):
    shard = lax.psum_scatter(value, "narrow", scatter_dimension=0, tiled=True)
    return lax.psum(shard, "wide").astype(f32)


def plain_sums(core, chunks):
    whole = []
    for keep, *send in chunks:
        send = jnp.concatenate(send)
        first = jnp.where(core == 0, keep, send)
        second = jnp.where(core == 0, send, keep)
        whole.append((first.reshape(D, WIDE_COLS), second))
    grad_in = jnp.stack([whole[0][0].reshape(D, 2, 3 * TILE), whole[1][0].reshape(D, 2, 3 * TILE)], axis=2)
    grad_out = jnp.stack([whole[0][1], whole[1][1]]).reshape(2, 2, 8, 3, 16, 2, D)
    grad_out = grad_out.transpose(1, 0, 3, 2, 5, 4, 6).reshape(FF, D)
    crosses, keys = whole[2][0], whole[2][1].reshape(D, WIDE_COLS)
    front_half, back_half = whole[3][0], whole[3][1].reshape(D, WIDE_COLS)
    return [
        plain_sum(v)
        for v in (
            jnp.concatenate([front_half[:, D:], back_half], axis=1),
            front_half[:, :D],
            crosses[:, D:],
            keys,
            crosses[:, :D],
            grad_in.reshape(D, FF),
            grad_out,
        )
    ]


def local(
    hidden_in, image_tokens, image_group, caption_len, norm_gain, norm_bias, self_qkv, self_out, cross_query,
    cross_kv, cross_out, mlp_in, mlp_bias_in, mlp_out, mlp_bias_out, out_grad,
):
    narrow = lax.axis_size("narrow")
    wide = lax.axis_size("wide")
    images, toks, _ = image_tokens.shape
    mine = images // narrow
    caps = 2 * mine
    rows = caps * SEQ
    n_at, w_at = lax.axis_index("narrow"), lax.axis_index("wide")
    fast = narrow == 2 and wide == 16
    core = w_at % 2
    if fast:
        flip = n_at * 8 + (w_at // 2) % 2 * 4 + (w_at // 4) % 2 * 2 + (w_at // 8) % 2
    else:
        flip = jnp.zeros_like(n_at)
    pos = jnp.stack([n_at, w_at * images, flip, core]).astype(jnp.int32)
    plan = make_plan(narrow, images, image_group, caption_len, pos)
    if narrow == 2:
        own, away = pick_tokens(plan, image_tokens, mine)
        got = swap(away, "narrow", 1)
        own = own.reshape(mine * toks, D)
        other = got.reshape(mine * toks, D)
    else:
        every = lax.all_gather(image_tokens, "narrow")
        first = n_at * mine
        tokens = lax.dynamic_slice_in_dim(every, first, mine, 1).transpose(1, 0, 2, 3)
        own, other = None, tokens.reshape(mine * IMG_TOK, D)
    x, attn, qkv, self_probs, self_mix, one, cin, cq, kv_own = front(
        rows, plan, hidden_in, out_grad, norm_gain, norm_bias, self_qkv, self_out, cross_query, own, cross_kv
    )
    kv, cross_probs, cross_mix, two, min_, g = cross(
        plan, kv_own, other, cq, one, norm_gain, norm_bias, cross_kv, cross_out, out_grad
    )
    state = {}
    token = min_

    def first_half(tie):
        acc, gn, bias, *chunk = mlp(0, plan, min_, g, None, None, mlp_in, mlp_bias_in, mlp_out)
        state.update(acc=acc, gn=gn, bias0=bias, a=chunk)
        return bias

    def second_half(tie):
        acc, gn = tie(state["acc"], state["gn"])
        acc, gn, bias, *chunk = mlp(1, plan, min_, g, acc, gn, mlp_in, mlp_bias_in, mlp_out)
        state.update(acc=acc, gn=gn, bias1=bias, b=chunk)
        return bias

    def cross_one(tie):
        acc, gn = tie(state["acc"], state["gn"])
        hidden_out, gtwo, gcross, gcq, gkv, small = cross_scores_back(
            acc, gn, two, g, norm_gain, mlp_bias_out, cross_out, cross_mix, cross_probs, kv, cq
        )
        state.update(hidden_out=hidden_out, gtwo=gtwo, gcross=gcross, gcq=gcq, gkv=gkv, small2=small)
        return small

    def cross_two(tie):
        gcq, gkv = tie(state["gcq"], state["gkv"])
        gone, gimg, small, *chunk = cross_weights_back(
            plan, state["gcross"], gcq, gkv, state["gtwo"], one, norm_gain, cross_query, cross_kv, cin, own, other
        )
        state.update(gone=gone, gimg=gimg, small1=small, c=chunk)
        return small

    def self_one(tie):
        gone, low_ = tie(state["gone"], self_mix)
        gself, gqkv = self_scores_back(gone, qkv, self_probs, low_, self_out)
        state.update(gself=gself, gqkv=gqkv)
        return gself

    def self_two(tie):
        gself, gqkv = tie(state["gself"], state["gqkv"])
        grad_hidden, small, *chunk = self_weights_back(
            plan, gself, gqkv, state["gone"], x, attn, norm_gain, self_qkv, state["small1"], state["small2"],
            (state["bias0"], state["bias1"]),
        )
        state.update(grad_hidden=grad_hidden, d=chunk, s=small)
        return small

    def place_out(got):
        return place(OUT_SRC, caps, plan, state["hidden_out"], got, bf16, "place_out")

    def place_grad(got):
        return place(OUT_SRC, caps, plan, state["grad_hidden"], got, f32, "place_grad")

    def place_image(got):
        return place(IMG_SRC, images, plan, state["gimg"].reshape(mine, IMG_TOK, D)[:, :toks], got, f32, "place_image")

    def finish_two(token):
        return finish_mlp(plan, live["a"].done(token), live["b"].done(token))

    def finish_cross(token):
        cuts = (((0, 0, 0, D), (1, D, 0, D)), ((2, 0, 0, 2 * D),))
        return finish_columns(plan, live["c"].done(token), cuts, (D, D, 2 * D), "finish_cross")

    def finish_self(token):
        cuts = (((0, 0, 0, D), (1, D, 0, D)), ((1, 0, D, 2 * D),))
        return finish_columns(plan, live["d"].done(token), cuts, (D, 3 * D), "finish_self")

    live = {}
    last = {"Fm": finish_two, "Fc": finish_cross, "Fd": finish_self}
    kernels = {
        "K0": first_half, "K1": second_half, "K2": cross_one, "K3": cross_two, "K4": self_one, "K5": self_two
    }
    if fast:
        for event in ORDER:
            if event in kernels:
                token = kernels[event](functools.partial(after, token))
                for name in "abcd":
                    if name in state:
                        live[name] = Chunk(*state.pop(name), parts=PARTS.get(name))
                if event == "K2":
                    away = state["hidden_out"].reshape(mine, 2, SEQ, D)[:, 1]
                    live["Ph"] = Away(away, place_out)
                if event == "K3":
                    away = state["gimg"].reshape(mine, IMG_TOK, D)[:, toks:].astype(bf16)
                    live["Pi"] = Away(away, place_image)
                if event == "K5":
                    away = state["grad_hidden"].reshape(mine, 2, SEQ, D)[:, 1].astype(bf16)
                    live["Pg"] = Away(away, place_grad)
                    live["s"] = Small(state.pop("s"))
            elif event in last:
                state[event] = last[event](token)
                token = state[event]
            else:
                token = together(token, [live[name] for name in event.split("+")])
        final_out, final_grad, grad_image = (live[name].out for name in ("Ph", "Pg", "Pi"))
        grad_mlp_in, grad_mlp_out = state["Fm"]
        grad_cross_out, grad_query, grad_kv = state["Fc"]
        grad_self_out, grad_qkv = state["Fd"]
        small = live["s"].keep
    else:
        for kernel in kernels.values():
            kernel(lambda *values: values)
        grad_qkv, grad_self_out, grad_query, grad_kv, grad_cross_out, grad_mlp_in, grad_mlp_out = plain_sums(
            core, [state[name] for name in "abcd"]
        )
        small = lax.psum(state["s"], ("wide", "narrow"))
        out_all = lax.all_gather(state["hidden_out"], "narrow", tiled=True)
        grad_all = lax.all_gather(state["grad_hidden"].astype(bf16), "narrow", tiled=True)
        final_out = place(OUT_SRC, caps, plan, out_all, out_all[:1], bf16, "place_out")
        final_grad = place(OUT_SRC, caps, plan, grad_all, grad_all[:1], f32, "place_grad")
        every = lax.all_gather(state["gimg"].reshape(mine, IMG_TOK, D).astype(bf16), "narrow", tiled=True)
        grad_image = lax.dynamic_slice_in_dim(every, n_at * toks, toks, 1).astype(f32)
    share = D // narrow
    columns = lax.dynamic_slice_in_dim(small[:7], n_at * share, share, 1)
    grad_bias_in = lax.dynamic_slice_in_dim(small[7:11].reshape(FF), n_at * (FF // narrow), FF // narrow, 0)
    return (
        final_out.reshape(rows, D),
        final_grad.reshape(rows, D),
        grad_image,
        columns[:3],
        columns[3:6],
        grad_qkv,
        grad_self_out,
        grad_query,
        grad_kv,
        grad_cross_out,
        grad_mlp_in,
        grad_bias_in,
        grad_mlp_out,
        columns[6],
    )


def solution(mesh):
    in_specs = (
        P("wide", None),
        P("wide", "narrow", None),
        P("wide"),
        P("wide"),
    ) + (P(),) * 11 + (P("wide", None),)
    out_specs = (
        P(("wide", "narrow"), None),
        P(("wide", "narrow"), None),
        P("wide", "narrow", None),
        P(None, "narrow"),
        P(None, "narrow"),
        P("narrow", None),
        P("narrow", None),
        P("narrow", None),
        P("narrow", None),
        P("narrow", None),
        P("narrow", None),
        P("narrow"),
        P("narrow", None),
        P("narrow"),
    )
    return jax.shard_map(local, mesh=mesh, in_specs=in_specs, out_specs=out_specs, check_vma=False)
```
